512 devices in a mesh: grow: 16 (over x, y), gcol: 32 (over z, core).
Axes of the slice: x: 4, y: 4, z: 16, core: 2. Of those that a mesh axis runs over, the one named last changes fastest.
Arguments:
- pair_matrix: bfloat16 [3, 2, 16384, 512], P(None, None, 'grow', 'gcol'), may hold values from -2 to 2
- valence_index: int32 [3, 512], replicated, may hold values from 0 to 2047
- conduction_index: int32 [3, 512], replicated, may hold values from 0 to 2047
- valence_energy: float32 [2048], replicated, may hold values from -12 to 0
- conduction_energy: float32 [2048], replicated, may hold values from 0.5 to 20
Outputs:
- chi: float32 [2, 16384, 16384], P(None, 'grow', 'gcol')
The draws below stay inside these ranges and needn't reach their ends.
All inputs are finite; a program needn't handle non-finite values.
Results may differ from the reference program's by a relative error of at most 0.0028.
Values may be sent and summed in bfloat16 or wider, within the bound.
A program may use at most 64 MiB of HBM per device.

```python
import jax
import jax.numpy as jnp

NG = 16384
NP = 512
PANELS = 3
NV = 2048
NC = 2048


def plant(result, key, low, high):
    extent = result.shape
    spot = [jax.random.randint(jax.random.fold_in(key, axis), (), 0, extent[axis]) for axis in range(len(extent))]
    result = result.at[tuple(spot)].set(low)
    longest = extent.index(max(extent))
    spot[longest] = (spot[longest] + 1) % extent[longest]
    return result.at[tuple(spot)].set(high)


def level_of(stream_key, dims, pieces, least, top_value):
    level = 1.0
    for axis_at, blocks in pieces:
        steps = jax.random.uniform(jax.random.fold_in(jax.random.fold_in(stream_key, 6), axis_at), (blocks,), jnp.float32, least / len(pieces), top_value / len(pieces))
        level = level * jnp.repeat(jnp.exp(steps), dims[axis_at] // blocks).reshape((-1,) + (1,) * (len(dims) - 1 - axis_at))
    return level


def normal_values(own_key, shape, spread, reach, split=(), held_as=jnp.bfloat16):
    factor_of = level_of(own_key, shape, split, -0.22, 0.18) if split else 1.0
    values = jax.random.normal(own_key, shape, jnp.float32) * spread * factor_of
    return jnp.minimum(jnp.maximum(values, -reach), reach).astype(held_as)


def setup_inputs(seed: int = 0) -> dict:
    splits = jax.random.split(jax.random.key(seed), 6)
    pair_matrix = normal_values(splits[0], (PANELS, 2, NG, NP), 0.125, 2.0, ((2, 16), (3, 32)))
    valence_index = plant(jax.random.randint(splits[1], (PANELS, NP), 0, NV), jax.random.fold_in(splits[1], 1), 0, NV - 1).astype(jnp.int32)
    conduction_index = plant(jax.random.randint(splits[2], (PANELS, NP), 0, NC), jax.random.fold_in(splits[2], 1), 0, NC - 1).astype(jnp.int32)
    valence_energy = jnp.clip(jax.random.uniform(splits[3], (NV,), jnp.float32, -12.0, 0.0), -12.0, 0.0)
    conduction_energy = jnp.clip(jax.random.uniform(splits[4], (NC,), jnp.float32, 0.5, 20.0), 0.5, 20.0)
    return {"pair_matrix": pair_matrix, "valence_index": valence_index, "conduction_index": conduction_index, "valence_energy": valence_energy, "conduction_energy": conduction_energy}


def reference(pair_matrix, valence_index, conduction_index, valence_energy, conduction_energy):
    weight = 2.0 / (valence_energy[valence_index] - conduction_energy[conduction_index])
    real_part = jnp.zeros((NG, NG), jnp.float32)
    imag_part = jnp.zeros((NG, NG), jnp.float32)
    for panel in range(PANELS):
        mat_real = pair_matrix[panel, 0]
        mat_imag = pair_matrix[panel, 1]
        scale = weight[panel][None, :]
        blk_real = (mat_real.astype(jnp.float32) * scale).astype(jnp.bfloat16)
        blk_imag = (-(mat_imag.astype(jnp.float32)) * scale).astype(jnp.bfloat16)
        real_part = real_part + jnp.dot(mat_real, blk_real.T, preferred_element_type=jnp.float32) - jnp.dot(mat_imag, blk_imag.T, preferred_element_type=jnp.float32)
        imag_part = imag_part + jnp.dot(mat_real, blk_imag.T, preferred_element_type=jnp.float32) + jnp.dot(mat_imag, blk_real.T, preferred_element_type=jnp.float32)
    return jnp.stack([real_part, imag_part])
```

```python
import functools

import jax
import jax.numpy as jnp
from jax import lax
from jax.experimental import pallas as pl
from jax.experimental.pallas import tpu as pltpu
from jax.sharding import PartitionSpec as P

MESH = pl.DeviceIdType.MESH
SIDE = 4
DEEP = 16
SUB = 32
LAST = 26
HOP = 2
ROWS = 256

TREE = {
    (1, 0): (1, 0), (3, 0): (3, 0), (2, 0): (1, 0), (1, 2): (0, 2), (3, 1): (0, 1), (3, 3): (0, 3),
    (1, 1): (0, 3), (1, 3): (0, 1), (2, 3): (0, 3), (3, 2): (0, 1), (2, 1): (3, 0), (0, 3): (1, 0),
    (0, 1): (1, 0), (0, 2): (3, 0), (2, 2): (1, 0),
}
STEPS = [(1, 0), (3, 0), (0, 1), (0, 3), (0, 2), (2, 0)]


def node_depth(node):
    depth = 0
    while node != (0, 0):
        step = TREE[node]
        node = ((node[0] - step[0]) % SIDE, (node[1] - step[1]) % SIDE)
        depth += 1
    return depth


def tree_tables():
    masks, depths, slots = {}, 0, {}
    count = [0] * (SIDE * SIDE)
    for step in STEPS:
        for node, used in sorted(TREE.items()):
            if used == step:
                parent = ((node[0] - step[0]) % SIDE, (node[1] - step[1]) % SIDE)
                place = parent[0] * SIDE + parent[1]
                slots.setdefault(step, [0] * (SIDE * SIDE))[place] = count[place]
                masks[step] = masks.get(step, 0) | (1 << place)
                count[place] += 1
    for node in TREE:
        depths |= node_depth(node) << (2 * (node[0] * SIDE + node[1]))
    lanes = {s: sum(v << (2 * p) for p, v in enumerate(slots[s])) for s in slots}
    signed = lambda v: v - (1 << 32) if v >= (1 << 31) else v
    return masks, signed(depths), {s: signed(v) for s, v in lanes.items()}, max(count)


MASKS, DEPTHS, LANES, MOST = tree_tables()


def turn(step, times):
    for _ in range(times):
        step = ((-step[1]) % SIDE, step[0] % SIDE)
    return step


def slot_of(s, way, core):
    return jnp.where(s == 0, core, 4 * s - 2 + jnp.where(s == 8, 0, 2 * way) + core)


def far_part(way, sub, core):
    return (sub == 2 * way) | ((sub == 1) & (core == way))


def kernel(x_ref, vi_ref, ci_ref, ve_ref, ce_ref, out_ref, rows_buf, cols_buf, rhs, acc, wcol, ibuf,
           zsend, zrecv, dsend, drecv, csend, crecv, osem):
    g = lax.axis_index("grow")
    gc = lax.axis_index("gcol")
    x, y, z, c = g // SIDE, g % SIDE, gc // 2, gc % 2
    dx, dy = (x - z // SIDE + SIDE) % SIDE, (y - z % SIDE + SIDE) % SIDE
    is_root = (dx == 0) & (dy == 0)

    def plane(step, core):
        return {"grow": ((x + step[0]) % SIDE) * SIDE + (y + step[1]) % SIDE, "gcol": z * 2 + core}

    def along(way):
        return {"grow": g, "gcol": ((z + (1 if way == 0 else DEEP - 1)) % DEEP) * 2 + c}

    sibling = {"grow": g, "gcol": z * 2 + 1 - c}

    barrier = pltpu.get_barrier_semaphore()
    others = [along(0), along(1), sibling] + [plane(s, k) for s in STEPS for k in range(2)]
    for other in others:
        pl.semaphore_signal(barrier, inc=1, device_id=other, device_id_type=MESH)
    rows_buf[c] = x_ref[...]
    pl.semaphore_wait(barrier, len(others))

    def piece(i):
        return i // 3, i % 3

    def zcopy(way, i):
        s, sub = piece(i)
        at = pl.ds(pl.multiple_of(sub * SUB, SUB), SUB)
        return pltpu.make_async_remote_copy(
            src_ref=rows_buf.at[slot_of(s, way, c), at],
            dst_ref=rows_buf.at[slot_of(s + 1, way, c), at],
            send_sem=zsend.at[way, i], recv_sem=zrecv.at[way, i + 3],
            device_id=along(way), device_id_type=MESH)

    def zsends(way, i):
        s, sub = piece(i)
        return (s < 7) | ((s == 7) & far_part(way, sub, c))

    def dcopy(slot):
        return pltpu.make_async_remote_copy(
            src_ref=rows_buf.at[slot], dst_ref=rows_buf.at[slot],
            send_sem=dsend.at[slot], recv_sem=drecv.at[slot],
            device_id=sibling, device_id_type=MESH)

    def cvalid(way, core, i):
        s, sub = piece(i)
        return ((s == 0) & (way == 0)) | ((s > 0) & (s < 8)) | ((s == 8) & far_part(way, sub, core))

    def root_copies(way, core, i):
        s, sub = piece(i)
        slot = slot_of(s, way, core)
        at = pl.ds(pl.multiple_of(sub * SUB, SUB), SUB)
        tree = 2 * way + core
        copies = []
        for n, step in enumerate(s for s in STEPS if MASKS.get(s, 0) & 1):
            for half in range(2):
                copies.append(pltpu.make_async_remote_copy(
                    src_ref=rows_buf.at[slot, at, half * 512:(half + 1) * 512],
                    dst_ref=cols_buf.at[slot, at],
                    send_sem=csend.at[tree, i, 2 * n + half], recv_sem=crecv.at[tree, i],
                    device_id=plane(turn(step, tree), half), device_id_type=MESH))
        return copies

    def place_in(tree):
        px, py = dx, dy
        for _ in range(tree):
            px, py = py, (SIDE - px) % SIDE
        return px * SIDE + py

    places = [place_in(t) for t in range(4)]
    lags = [HOP * ((DEPTHS >> (2 * places[t])) & 3) for t in range(4)]

    def ccopy(tree, i, step):
        s, sub = piece(i)
        slot = slot_of(s, tree // 2, tree % 2)
        at = pl.ds(pl.multiple_of(sub * SUB, SUB), SUB)
        lane = (LANES[step] >> (2 * places[tree])) & 3
        return pltpu.make_async_remote_copy(
            src_ref=cols_buf.at[slot, at], dst_ref=cols_buf.at[slot, at],
            send_sem=csend.at[tree, i, lane], recv_sem=crecv.at[tree, i],
            device_id=plane(turn(step, tree), c), device_id_type=MESH)

    def passes(tree, step):
        return ((MASKS[step] >> places[tree]) & 1) == 1

    def z_turn(i):
        s, sub = piece(i)
        for way in range(2):
            have = ((s > 0) & (s < 8)) | ((s == 8) & far_part(way, sub, c))

            @pl.when(have)
            def _():
                zcopy(way, i - 3).wait_recv()

            @pl.when(zsends(way, i))
            def _():
                zcopy(way, i).start()

            for core in range(2):
                @pl.when(is_root & (c == core) & cvalid(way, core, i))
                def _():
                    for copy in root_copies(way, core, i):
                        copy.start()

            @pl.when((sub == 2) & (s > 0) & (s < 8))
            def _():
                dcopy(slot_of(s, way, c)).start()

        @pl.when(i == LAST)
        def _():
            dcopy(30 + c).start()

    def c_turn(i):
        for tree in range(4):
            j = i - lags[tree]

            @pl.when((j >= 0) & (j <= LAST) & cvalid(tree // 2, tree % 2, j))
            def _():
                ccopy(tree, j, STEPS[0]).wait_recv()
                for step in STEPS:
                    if step in MASKS:
                        @pl.when(passes(tree, step))
                        def _():
                            ccopy(tree, j, step).start()

    def drain(i):
        for way in range(2):
            @pl.when(zsends(way, i))
            def _():
                zcopy(way, i).wait_send()

            for core in range(2):
                @pl.when(is_root & (c == core) & cvalid(way, core, i))
                def _():
                    for copy in root_copies(way, core, i):
                        copy.wait_send()
        for tree in range(4):
            @pl.when(jnp.logical_not(is_root) & cvalid(tree // 2, tree % 2, i))
            def _():
                for step in STEPS:
                    if step in MASKS:
                        @pl.when(passes(tree, step))
                        def _():
                            ccopy(tree, i, step).wait_send()

    def weights():
        def look(table, index):
            out = []
            for j in range(4):
                at = index[:, j * 128:(j + 1) * 128]
                low, high = at & 127, at >> 7
                value = jnp.zeros((8, 128), jnp.float32)
                for r in range(16):
                    row = jnp.broadcast_to(table[r:r + 1, :], (8, 128))
                    value = jnp.where(high == r, jnp.take_along_axis(row, low, axis=1), value)
                out.append(value)
            return out

        ibuf[...] = jnp.zeros_like(ibuf)
        ibuf[0, 0:3, :] = vi_ref[...]
        ibuf[1, 0:3, :] = ci_ref[...]
        low = look(ve_ref, ibuf[0])
        high = look(ce_ref, ibuf[1])
        for j in range(4):
            w = 2.0 / (low[j] - high[j])
            for k in range(3):
                wcol[k, j * 128:(j + 1) * 128, :] = jnp.broadcast_to(w[k:k + 1, :], (128, 128)).T

    def build(first, count):
        def arrived(q):
            @pl.when(q % 2 != c)
            def _():
                dcopy(q).wait_recv()

        def fill(load):
            @pl.loop(0, count)
            def _(n):
                q = first + n
                s, way, core = (q + 2) // 4, ((q + 2) % 4) // 2, q % 2
                chip = (z + jnp.where(way == 1, s, DEEP - s)) % DEEP
                band = pl.multiple_of((2 * chip + core) * 16, 16)
                base = n * 96
                for k in range(3):
                    w = wcol[k, pl.ds(band, 16), :]
                    w = jnp.concatenate([w] * 4, axis=1)
                    re = (load(q, 32 * k).astype(jnp.float32) * w).astype(jnp.bfloat16)
                    im = (load(q, 32 * k + 16).astype(jnp.float32) * w).astype(jnp.bfloat16)
                    top = pl.ds(pl.multiple_of(base + 32 * k, 16), 16)
                    low = pl.ds(pl.multiple_of(base + 32 * k + 16, 16), 16)
                    rhs[top, 0:512] = re
                    rhs[low, 0:512] = im
                    rhs[top, 512:1024] = -im
                    rhs[low, 512:1024] = re

        @pl.loop(0, count)
        def _(n):
            arrived(first + n)

        @pl.when(is_root)
        def _():
            half = pl.ds(pl.multiple_of(c * 512, 512), 512)
            fill(lambda q, r: rows_buf[q, r:r + 16, half])

        @pl.when(jnp.logical_not(is_root))
        def _():
            fill(lambda q, r: cols_buf[q, r:r + 16, :])

    def block(first, count, r, fresh):
        at = pl.ds(pl.multiple_of(r * ROWS, ROWS), ROWS)
        left = rows_buf[first:first + count, :, at].reshape(count * 96, ROWS)
        value = lax.dot_general(left, rhs[0:count * 96, :], (((0,), (0,)), ((), ())),
                                preferred_element_type=jnp.float32)
        if fresh:
            acc[at, :] = value
        else:
            acc[at, :] += value

    def write(r):
        at = pl.ds(pl.multiple_of(r * ROWS, ROWS), ROWS)
        return [pltpu.make_async_copy(acc.at[at, part * 512:(part + 1) * 512], out_ref.at[part, at], osem.at[part, r])
                for part in range(2)]

    blocks = 1024 // ROWS
    groups = [(0, 6), (6, 8), (14, 8), (22, 8), (30, 2)]
    slack = 3 * HOP
    ready = [3 * s + 2 + slack for s in (1, 3, 5, 7)]

    z_turn(jnp.int32(0))
    z_turn(jnp.int32(1))
    z_turn(jnp.int32(2))
    dcopy(c).start()
    weights()

    @pl.loop(0, LAST + slack + 1)
    def _(i):
        @pl.when((i > 2) & (i <= LAST))
        def _():
            z_turn(i)

        @pl.when(jnp.logical_not(is_root))
        def _():
            c_turn(i)

        for n, begin in enumerate(ready):
            first, count = groups[n]

            @pl.when(i == begin)
            def _():
                build(first, count)

            @pl.when((i >= begin) & (i < begin + blocks))
            def _():
                block(first, count, i - begin, n == 0)

        @pl.when(i >= slack + 3)
        def _():
            drain(i - slack - 3)

    build(*groups[4])

    @pl.loop(0, blocks)
    def _(r):
        block(groups[4][0], groups[4][1], r, False)
        for copy in write(r):
            copy.start()

    @pl.loop(LAST - 2, LAST + 1)
    def _(i):
        drain(i)

    @pl.loop(0, 32)
    def _(q):
        @pl.when(q % 2 == c)
        def _():
            dcopy(q).wait_send()

    @pl.loop(0, blocks)
    def _(r):
        for copy in write(r):
            copy.wait()


def shards(pair_matrix, valence_index, conduction_index, valence_energy, conduction_energy):
    x = jnp.swapaxes(pair_matrix, 2, 3).reshape(96, 1024)
    vmem = pl.BlockSpec(memory_space=pltpu.VMEM)
    return pl.pallas_call(
        kernel,
        out_shape=jax.ShapeDtypeStruct((2, 1024, 512), jnp.float32),
        in_specs=[vmem] * 5,
        out_specs=pl.BlockSpec(memory_space=pl.ANY),
        scratch_shapes=[
            pltpu.VMEM((32, 96, 1024), jnp.bfloat16),
            pltpu.VMEM((32, 96, 512), jnp.bfloat16),
            pltpu.VMEM((768, 1024), jnp.bfloat16),
            pltpu.VMEM((1024, 1024), jnp.float32),
            pltpu.VMEM((3, 512, 128), jnp.float32),
            pltpu.VMEM((2, 8, 512), jnp.int32),
            pltpu.SemaphoreType.DMA((2, LAST + 1)),
            pltpu.SemaphoreType.DMA((2, LAST + 1)),
            pltpu.SemaphoreType.DMA((32,)),
            pltpu.SemaphoreType.DMA((32,)),
            pltpu.SemaphoreType.DMA((4, LAST + 1, 4)),
            pltpu.SemaphoreType.DMA((4, LAST + 1)),
            pltpu.SemaphoreType.DMA((2, 1024 // ROWS)),
        ],
        compiler_params=pltpu.CompilerParams(collective_id=0, has_side_effects=True, vmem_limit_bytes=40 << 20),
        cost_estimate=pl.CostEstimate(flops=6 << 30, bytes_accessed=4 << 20, transcendentals=0),
        name="chi",
    )(x, valence_index, conduction_index, valence_energy.reshape(16, 128), conduction_energy.reshape(16, 128))


def solution(mesh):
    in_specs = (P(None, None, "grow", "gcol"), P(), P(), P(), P())
    out_specs = P(None, "grow", "gcol")
    return jax.shard_map(shards, mesh=mesh, in_specs=in_specs, out_specs=out_specs, check_vma=False)
```

```python
import functools

import jax
import jax.numpy as jnp
from jax import lax
from jax.experimental import pallas as pl
from jax.experimental.pallas import tpu as pltpu
from jax.sharding import PartitionSpec as P

MESH = pl.DeviceIdType.MESH
SIDE = 4
DEEP = 16
SUB = 32
LAST = 26
HOP = 2
ROWS = 512

TREES = [
    {
        (1, 0): (0, 1), (1, 3): (1, 0), (2, 3): (0, 3), (2, 1): (0, 3), (0, 1): (0, 3), (1, 2): (0, 3),
        (0, 3): (0, 3), (3, 3): (3, 0), (3, 0): (0, 1), (2, 2): (3, 0), (3, 2): (0, 3), (1, 1): (0, 3),
        (0, 2): (3, 0), (2, 0): (3, 0), (3, 1): (0, 3),
    },
    {
        (1, 0): (1, 0), (3, 0): (3, 0), (2, 0): (1, 0), (1, 2): (0, 2), (3, 1): (0, 1), (3, 3): (0, 3),
        (1, 1): (0, 3), (1, 3): (0, 1), (2, 3): (0, 3), (3, 2): (0, 1), (2, 1): (3, 0), (0, 3): (1, 0),
        (0, 1): (1, 0), (0, 2): (3, 0), (2, 2): (1, 0),
    },
]
SPLIT = 20
STEPS = [(1, 0), (3, 0), (0, 1), (0, 3), (0, 2), (2, 0)]


def children_of(tree, node):
    return [s for s in STEPS if tree.get(((node[0] + s[0]) % SIDE, (node[1] + s[1]) % SIDE)) == s]


def node_depth(tree, node):
    depth = 0
    while node != (0, 0):
        step = tree[node]
        node = ((node[0] - step[0]) % SIDE, (node[1] - step[1]) % SIDE)
        depth += 1
    return depth


NODES = [(px, py) for px in range(SIDE) for py in range(SIDE)]
ROOT_FANS = [children_of(t, (0, 0)) for t in TREES]
FAN = max(len(children_of(t, n)) for t in TREES for n in NODES if n != (0, 0))
DEEPEST = [max(node_depth(t, n) for n in NODES) for t in TREES]


def pick(place, values):
    shift = max(max(values).bit_length(), 1)
    per = 31 // shift
    result = jnp.int32(0)
    for start in range(0, len(values), per):
        part = values[start:start + per]
        word = sum(v << (shift * n) for n, v in enumerate(part))
        if word:
            here = (place >= start) & (place < start + per)
            offset = jnp.where(here, place - start, 0) * shift
            result = result + jnp.where(here, (word >> offset) & ((1 << shift) - 1), 0)
    return result


def turn(step, times):
    for _ in range(times):
        step = ((-step[1]) % SIDE, step[0] % SIDE)
    return step


def piece(i):
    s = (i * 11) >> 5
    return s, i - 3 * s


def slot_of(s, way, core):
    if way == 0:
        return jnp.where(s == 0, core, 4 * s - 2 + core)
    return jnp.where(s == 0, core, jnp.where(s == 8, 30 + core, 4 * s + core))


def far_part(way, sub, core):
    return (sub == 2 * way) | ((sub == 1) & (core == way))


def kernel(x_hbm, vi_hbm, ci_hbm, ve_hbm, ce_hbm, out_ref, rows_buf, cols_buf, rhs, wcol, vi_ref, ci_ref, ve_ref, ce_ref, ibuf,
           isem, zsend, zrecv, dsend, drecv, csend, crecv):
    g = lax.axis_index("grow")
    gc = lax.axis_index("gcol")
    x, y, z, c = g // SIDE, g % SIDE, gc // 2, gc % 2
    dx, dy = (x - z // SIDE + SIDE) % SIDE, (y - z % SIDE + SIDE) % SIDE
    is_root = (dx == 0) & (dy == 0)

    parts = [(x_hbm.at[SUB * k:SUB * (k + 1), 512 * h:512 * (h + 1)], rows_buf.at[3 * c + k, h])
             for k in range(3) for h in range(2)]
    parts += [(vi_hbm, vi_ref), (ci_hbm, ci_ref), (ve_hbm, ve_ref), (ce_hbm, ce_ref)]
    loads = [pltpu.make_async_copy(src, dst, isem.at[max(n - 5, 0)]) for n, (src, dst) in enumerate(parts)]
    for load in loads:
        load.start()

    def grow_at(step):
        return ((x + step[0]) % SIDE) * SIDE + (y + step[1]) % SIDE

    def dev(grow, gcol):
        return {"grow": grow, "gcol": gcol}

    ends = [((z + 1) % DEEP) * 2 + c, ((z + DEEP - 1) % DEEP) * 2 + c]
    sibling = dev(g, z * 2 + 1 - c)

    barrier = pltpu.get_barrier_semaphore()
    others = [dev(g, ends[0]), dev(g, ends[1]), sibling]
    others += [dev(grow_at(s), z * 2 + k) for s in STEPS for k in range(2)]
    for other in others:
        pl.semaphore_signal(barrier, inc=1, device_id=other, device_id_type=MESH)

    depths, fans, kids = [[], []], [[], []], [[], []]

    def find_roles():
        px, py = dx, dy
        for tree in range(4):
            place = px * SIDE + py
            for kind, table in enumerate(TREES):
                depths[kind].append(pick(place, [node_depth(table, n) for n in NODES]))
                lists = [children_of(table, n) if n != (0, 0) else [] for n in NODES]
                fans[kind].append(pick(place, [len(v) for v in lists]))
                mine = []
                for n in range(FAN):
                    codes = [STEPS.index(v[n]) if n < len(v) else 0 for v in lists]
                    code = pick(place, codes)
                    chip = jnp.int32(0)
                    for k in sorted(set(codes)):
                        chip = jnp.where(code == k, grow_at(turn(STEPS[k], tree)), chip)
                    mine.append(chip)
                kids[kind].append(mine)
            px, py = py, (SIDE - px) % SIDE

    def arrival(ref, sem):
        pltpu.make_async_copy(ref, ref, sem).wait()

    def zcopy(way, i):
        s, sub = piece(i)
        return pltpu.make_async_remote_copy(
            src_ref=rows_buf.at[3 * slot_of(s, way, c) + sub],
            dst_ref=rows_buf.at[3 * slot_of(s + 1, way, c) + sub],
            send_sem=zsend.at[0], recv_sem=zrecv.at[way, i],
            device_id=dev(g, ends[way]), device_id_type=MESH)

    def dcopy(slot):
        return pltpu.make_async_remote_copy(
            src_ref=rows_buf.at[pl.ds(3 * slot, 3)], dst_ref=rows_buf.at[pl.ds(3 * slot, 3)],
            send_sem=dsend.at[0], recv_sem=drecv.at[(slot + 2) >> 3],
            device_id=sibling, device_id_type=MESH)

    def root_copies(kind, way, i):
        s, sub = piece(i)
        slot = slot_of(s, way, c)
        tree = 2 * way + c
        copies = []
        for n, step in enumerate(ROOT_FANS[kind]):
            chip = jnp.where(c == 0, grow_at(turn(step, 2 * way)), grow_at(turn(step, 2 * way + 1)))
            for half in range(2):
                copies.append(pltpu.make_async_remote_copy(
                    src_ref=rows_buf.at[3 * slot + sub, half],
                    dst_ref=cols_buf.at[3 * slot + sub],
                    send_sem=csend.at[kind, tree, 2 * n + half], recv_sem=crecv.at[tree, i],
                    device_id=dev(chip, z * 2 + half), device_id_type=MESH))
        return copies

    def ccopy(kind, tree, i, n):
        s, sub = piece(i)
        slot = slot_of(s, tree // 2, tree % 2)
        return pltpu.make_async_remote_copy(
            src_ref=cols_buf.at[3 * slot + sub], dst_ref=cols_buf.at[3 * slot + sub],
            send_sem=csend.at[kind, tree, n], recv_sem=crecv.at[tree, i],
            device_id=dev(kids[kind][tree][n], gc), device_id_type=MESH)

    def z_turn(i, own=False):
        s, sub = piece(i)
        far = [far_part(way, sub, c) for way in range(2)]
        for way in range(2):
            if not own:
                @pl.when((s < 8) | far[way])
                def _():
                    zcopy(way, i - 3).wait_recv()

            @pl.when((s < 7) | ((s == 7) & far[way]))
            def _():
                zcopy(way, i).start()

        @pl.when(is_root)
        def _():
            for kind in range(2):
                @pl.when((i <= SPLIT) if kind == 0 else (i > SPLIT))
                def _():
                    for way in range(1 if own else 2):
                        if kind == 0:
                            for copy in root_copies(kind, way, i):
                                copy.start()
                        else:
                            @pl.when((s < 8) | far[way])
                            def _():
                                for copy in root_copies(kind, way, i):
                                    copy.start()

        if not own:
            @pl.when(sub == 2)
            def _():
                dcopy(slot_of(s, 0, c)).start()

                @pl.when(s < 8)
                def _():
                    dcopy(slot_of(s, 1, c)).start()

    def c_turn(kind, i):
        for tree in range(4):
            j = i - HOP * depths[kind][tree]
            if kind == 0:
                ok = (j >= 3 * (tree // 2)) & (j <= SPLIT)
            else:
                s, sub = piece(j)
                ok = (j > SPLIT) & ((s < 8) | ((j <= LAST) & far_part(tree // 2, sub, tree % 2)))

            @pl.when(ok)
            def _():
                ccopy(kind, tree, j, 0).wait_recv()

                def pass_on(n):
                    @pl.when(fans[kind][tree] > n)
                    def _():
                        ccopy(kind, tree, j, n).start()
                        if n + 1 < FAN:
                            pass_on(n + 1)

                pass_on(0)

    def drain(kind):
        def sent(tree, n, more):
            count = SPLIT + 1 - 3 * more if kind == 0 else 23 - SPLIT + more
            arrival(cols_buf.at[0:count], csend.at[kind, tree, n])

        @pl.when(is_root)
        def _():
            for way in range(2):
                for core in range(2):
                    @pl.when(c == core)
                    def _():
                        for n in range(2 * len(ROOT_FANS[kind])):
                            sent(2 * way + core, n, way if kind == 0 else 1 + (way == core))

        @pl.when(jnp.logical_not(is_root))
        def _():
            for tree in range(4):
                way, core = tree // 2, tree % 2
                for n in range(FAN):
                    @pl.when(fans[kind][tree] > n)
                    def _():
                        sent(tree, n, way if kind == 0 else 1 + (way == core))

    def drain_rows():
        arrival(rows_buf.at[0:45], zsend.at[0])
        arrival(rows_buf.at[0:48], dsend.at[0])

    def weights(j):
        lanes = pl.ds(pl.multiple_of(j * 128, 128), 128)

        def look(table, index):
            low, high = index & 127, index >> 7
            value = jnp.zeros((8, 128), jnp.float32)
            for r in range(16):
                row = jnp.broadcast_to(table[r:r + 1, :], (8, 128))
                value = jnp.where(high == r, jnp.take_along_axis(row, low, axis=1), value)
            return value

        @pl.when(j == 0)
        def _():
            for load in loads[6:]:
                load.wait()
            ibuf[...] = jnp.zeros_like(ibuf)
            ibuf[0, 0:3, :] = vi_ref[...]
            ibuf[1, 0:3, :] = ci_ref[...]

        w = 2.0 / (look(ve_ref, ibuf[0, :, lanes]) - look(ce_ref, ibuf[1, :, lanes]))
        for k in range(3):
            wcol[k, lanes, :] = jnp.broadcast_to(w[k:k + 1, :], (128, 128)).T

    def build(first, count):
        def fill(load):
            @pl.loop(0, count)
            def _(n):
                q = first + n
                s, way, core = (q + 2) // 4, ((q + 2) % 4) // 2, q % 2
                chip = (z + jnp.where(way == 1, s, DEEP - s)) % DEEP
                band = pl.multiple_of((2 * chip + core) * 16, 16)
                base = n * 96
                for k in range(3):
                    w = wcol[k, pl.ds(band, 16), :]
                    w = jnp.concatenate([w] * 4, axis=1)
                    re = (load(q, k, 0).astype(jnp.float32) * w).astype(jnp.bfloat16)
                    im = (load(q, k, 16).astype(jnp.float32) * w).astype(jnp.bfloat16)
                    top = pl.ds(pl.multiple_of(base + 32 * k, 16), 16)
                    low = pl.ds(pl.multiple_of(base + 32 * k + 16, 16), 16)
                    rhs[top, 0:512] = re
                    rhs[low, 0:512] = im
                    rhs[top, 512:1024] = -im
                    rhs[low, 512:1024] = re

        arrival(rows_buf.at[0:3 * count // 2], drecv.at[(first + 2) >> 3])

        @pl.when(is_root)
        def _():
            fill(lambda q, k, r: rows_buf[3 * q + k, c, r:r + 16, :])

        @pl.when(jnp.logical_not(is_root))
        def _():
            fill(lambda q, k, r: cols_buf[3 * q + k, r:r + 16, :])

    def block(first, count, r, fresh):
        at = pl.ds(pl.multiple_of(r * ROWS, ROWS), ROWS)
        left = rows_buf[3 * first:3 * (first + count), r].reshape(count * 96, ROWS)
        value = lax.dot_general(left, rhs[0:count * 96, :], (((0,), (0,)), ((), ())),
                                preferred_element_type=jnp.float32)
        for part in range(2):
            if fresh:
                out_ref[part, at, :] = value[:, part * 512:(part + 1) * 512]
            else:
                out_ref[part, at, :] += value[:, part * 512:(part + 1) * 512]

    blocks = 1024 // ROWS
    groups = [(0, 6), (6, 8), (14, 8), (22, 8), (30, 2)]
    depth0, depth1 = HOP * DEEPEST[0], HOP * DEEPEST[1]

    def ready(last_s):
        i = 3 * last_s + 2
        return i + depth0 if i <= SPLIT else max(SPLIT + depth0, i + depth1)

    begins = [ready(s) for s in (1, 3, 5, 7)]
    turns = LAST + depth1 + 1

    find_roles()
    arrival(rows_buf.at[pl.ds(3 * c, 3)], isem.at[0])
    pl.semaphore_wait(barrier, len(others))
    for i in range(3):
        z_turn(jnp.int32(i), own=True)
    dcopy(c).start()

    @pl.loop(0, turns)
    def _(i):
        @pl.when((i > 2) & (i <= LAST))
        def _():
            z_turn(i)

        @pl.when(jnp.logical_not(is_root))
        def _():
            @pl.when(i <= SPLIT + depth0)
            def _():
                c_turn(0, i)

            @pl.when(i > SPLIT)
            def _():
                c_turn(1, i)

        @pl.when((i >= 4) & (i < 8))
        def _():
            weights(i - 4)

        for n, begin in enumerate(begins):
            first, count = groups[n]

            @pl.when((i >= begin) & (i < begin + blocks))
            def _():
                @pl.when(i == begin)
                def _():
                    build(first, count)

                block(first, count, i - begin, n == 0)

    first, count = groups[4]
    build(first, count)

    @pl.loop(0, blocks)
    def _(r):
        block(first, count, r, False)

    drain(0)
    drain(1)
    drain_rows()


def shards(pair_matrix, valence_index, conduction_index, valence_energy, conduction_energy):
    x = jnp.swapaxes(pair_matrix, 2, 3).reshape(96, 1024)
    return pl.pallas_call(
        kernel,
        out_shape=jax.ShapeDtypeStruct((2, 1024, 512), jnp.float32),
        in_specs=[pl.BlockSpec(memory_space=pltpu.HBM)] * 5,
        out_specs=pl.BlockSpec(memory_space=pltpu.VMEM),
        scratch_shapes=[
            pltpu.VMEM((96, 2, SUB, 512), jnp.bfloat16),
            pltpu.VMEM((96, SUB, 512), jnp.bfloat16),
            pltpu.VMEM((768, 1024), jnp.bfloat16),
            pltpu.VMEM((3, 512, 128), jnp.float32),
            pltpu.VMEM((3, 512), jnp.int32),
            pltpu.VMEM((3, 512), jnp.int32),
            pltpu.VMEM((16, 128), jnp.float32),
            pltpu.VMEM((16, 128), jnp.float32),
            pltpu.VMEM((2, 8, 512), jnp.int32),
            pltpu.SemaphoreType.DMA((5,)),
            pltpu.SemaphoreType.DMA((1,)),
            pltpu.SemaphoreType.DMA((2, LAST - 2)),
            pltpu.SemaphoreType.DMA((1,)),
            pltpu.SemaphoreType.DMA((5,)),
            pltpu.SemaphoreType.DMA((2, 4, 4)),
            pltpu.SemaphoreType.DMA((4, LAST + 1)),
        ],
        compiler_params=pltpu.CompilerParams(collective_id=0, has_side_effects=True, vmem_limit_bytes=40 << 20),
        cost_estimate=pl.CostEstimate(flops=6 << 30, bytes_accessed=4 << 20, transcendentals=0),
        name="chi",
    )(x, valence_index, conduction_index, valence_energy.reshape(16, 128), conduction_energy.reshape(16, 128))


def solution(mesh):
    in_specs = (P(None, None, "grow", "gcol"), P(), P(), P(), P())
    out_specs = P(None, "grow", "gcol")
    return jax.shard_map(shards, mesh=mesh, in_specs=in_specs, out_specs=out_specs, check_vma=False)
```

```python
import functools

import jax
import jax.numpy as jnp
from jax import lax
from jax.experimental import pallas as pl
from jax.experimental.pallas import tpu as pltpu
from jax.sharding import PartitionSpec as P

MESH = pl.DeviceIdType.MESH
SIDE = 4
DEEP = 16
SUB = 32
LAST = 26
HOP = 3
ROWS = 512

TREES = [
    {
        (1, 0): (0, 1), (1, 3): (1, 0), (2, 3): (0, 3), (2, 1): (0, 3), (0, 1): (0, 3), (1, 2): (0, 3),
        (0, 3): (0, 3), (3, 3): (3, 0), (3, 0): (0, 1), (2, 2): (3, 0), (3, 2): (0, 3), (1, 1): (0, 3),
        (0, 2): (3, 0), (2, 0): (3, 0), (3, 1): (0, 3),
    },
    {
        (1, 0): (1, 0), (3, 0): (3, 0), (2, 0): (1, 0), (1, 2): (0, 2), (3, 1): (0, 1), (3, 3): (0, 3),
        (1, 1): (0, 3), (1, 3): (0, 1), (2, 3): (0, 3), (3, 2): (0, 1), (2, 1): (3, 0), (0, 3): (1, 0),
        (0, 1): (1, 0), (0, 2): (3, 0), (2, 2): (1, 0),
    },
]
SPLIT = 14
STEPS = [(1, 0), (3, 0), (0, 1), (0, 3), (0, 2), (2, 0)]


def children_of(tree, node):
    return [s for s in STEPS if tree.get(((node[0] + s[0]) % SIDE, (node[1] + s[1]) % SIDE)) == s]


def node_depth(tree, node):
    depth = 0
    while node != (0, 0):
        step = tree[node]
        node = ((node[0] - step[0]) % SIDE, (node[1] - step[1]) % SIDE)
        depth += 1
    return depth


NODES = [(px, py) for px in range(SIDE) for py in range(SIDE)]
ROOT_FANS = [children_of(t, (0, 0)) for t in TREES]
FAN = max(len(children_of(t, n)) for t in TREES for n in NODES if n != (0, 0))
DEEPEST = [max(node_depth(t, n) for n in NODES) for t in TREES]


def pick(place, values):
    shift = max(max(values).bit_length(), 1)
    per = 31 // shift
    result = jnp.int32(0)
    for start in range(0, len(values), per):
        part = values[start:start + per]
        word = sum(v << (shift * n) for n, v in enumerate(part))
        if word:
            here = (place >= start) & (place < start + per)
            offset = jnp.where(here, place - start, 0) * shift
            result = result + jnp.where(here, (word >> offset) & ((1 << shift) - 1), 0)
    return result


def turn(step, times):
    for _ in range(times):
        step = ((-step[1]) % SIDE, step[0] % SIDE)
    return step


def piece(i):
    s = (i * 11) >> 5
    return s, i - 3 * s


def slot_of(s, way, core):
    if way == 0:
        return jnp.where(s == 0, core, 4 * s - 2 + core)
    return jnp.where(s == 0, core, jnp.where(s == 8, 30 + core, 4 * s + core))


def far_part(way, sub, core):
    return (sub == 2 * way) | ((sub == 1) & (core == way))


def kernel(x_hbm, vi_hbm, ci_hbm, ve_hbm, ce_hbm, out_ref, rows_buf, cols_buf, rhs, wcol, vi_ref, ci_ref, ve_ref, ce_ref, ibuf,
           isem, zsend, zrecv, dsend, drecv, csend, crecv):
    g = lax.axis_index("grow")
    gc = lax.axis_index("gcol")
    x, y, z, c = g // SIDE, g % SIDE, gc // 2, gc % 2
    dx, dy = (x - z // SIDE + SIDE) % SIDE, (y - z % SIDE + SIDE) % SIDE
    is_root = (dx == 0) & (dy == 0)

    parts = [(x_hbm.at[SUB * k:SUB * (k + 1), 512 * h:512 * (h + 1)], rows_buf.at[3 * c + k, h])
             for k in range(3) for h in range(2)]
    parts += [(vi_hbm, vi_ref), (ci_hbm, ci_ref), (ve_hbm, ve_ref), (ce_hbm, ce_ref)]
    loads = [pltpu.make_async_copy(src, dst, isem.at[max(n - 5, 0)]) for n, (src, dst) in enumerate(parts)]
    for load in loads:
        load.start()

    def grow_at(step):
        return ((x + step[0]) % SIDE) * SIDE + (y + step[1]) % SIDE

    def dev(grow, gcol):
        return {"grow": grow, "gcol": gcol}

    ends = [((z + 1) % DEEP) * 2 + c, ((z + DEEP - 1) % DEEP) * 2 + c]
    sibling = dev(g, z * 2 + 1 - c)

    barrier = pltpu.get_barrier_semaphore()
    others = [dev(g, ends[0]), dev(g, ends[1]), sibling]
    others += [dev(grow_at(s), z * 2 + k) for s in STEPS for k in range(2)]
    for other in others:
        pl.semaphore_signal(barrier, inc=1, device_id=other, device_id_type=MESH)

    depths, fans, kids = [[], []], [[], []], [[], []]

    def find_roles():
        px, py = dx, dy
        for tree in range(4):
            place = px * SIDE + py
            for kind, table in enumerate(TREES):
                depths[kind].append(pick(place, [node_depth(table, n) for n in NODES]))
                lists = [children_of(table, n) if n != (0, 0) else [] for n in NODES]
                fans[kind].append(pick(place, [len(v) for v in lists]))
                mine = []
                for n in range(FAN):
                    codes = [STEPS.index(v[n]) if n < len(v) else 0 for v in lists]
                    code = pick(place, codes)
                    chip = jnp.int32(0)
                    for k in sorted(set(codes)):
                        chip = jnp.where(code == k, grow_at(turn(STEPS[k], tree)), chip)
                    mine.append(chip)
                kids[kind].append(mine)
            px, py = py, (SIDE - px) % SIDE

    def arrival(ref, sem):
        pltpu.make_async_copy(ref, ref, sem).wait()

    def zcopy(way, i):
        s, sub = piece(i)
        return pltpu.make_async_remote_copy(
            src_ref=rows_buf.at[3 * slot_of(s, way, c) + sub],
            dst_ref=rows_buf.at[3 * slot_of(s + 1, way, c) + sub],
            send_sem=zsend.at[0], recv_sem=zrecv.at[way, i],
            device_id=dev(g, ends[way]), device_id_type=MESH)

    def dcopy(slot):
        return pltpu.make_async_remote_copy(
            src_ref=rows_buf.at[pl.ds(3 * slot, 3)], dst_ref=rows_buf.at[pl.ds(3 * slot, 3)],
            send_sem=dsend.at[0], recv_sem=drecv.at[(slot + 2) >> 3],
            device_id=sibling, device_id_type=MESH)

    def root_copies(kind, way, i):
        s, sub = piece(i)
        slot = slot_of(s, way, c)
        tree = 2 * way + c
        copies = []
        for n, step in enumerate(ROOT_FANS[kind]):
            chip = jnp.where(c == 0, grow_at(turn(step, 2 * way)), grow_at(turn(step, 2 * way + 1)))
            for half in range(2):
                copies.append(pltpu.make_async_remote_copy(
                    src_ref=rows_buf.at[3 * slot + sub, half],
                    dst_ref=cols_buf.at[3 * slot + sub],
                    send_sem=csend.at[kind, tree, 2 * n + half], recv_sem=crecv.at[tree, i],
                    device_id=dev(chip, z * 2 + half), device_id_type=MESH))
        return copies

    def ccopy(kind, tree, i, n):
        s, sub = piece(i)
        slot = slot_of(s, tree // 2, tree % 2)
        return pltpu.make_async_remote_copy(
            src_ref=cols_buf.at[3 * slot + sub], dst_ref=cols_buf.at[3 * slot + sub],
            send_sem=csend.at[kind, tree, n], recv_sem=crecv.at[tree, i],
            device_id=dev(kids[kind][tree][n], gc), device_id_type=MESH)

    def z_turn(i, own=False):
        s, sub = piece(i)
        far = [far_part(way, sub, c) for way in range(2)]
        for way in range(2):
            if not own:
                @pl.when((s < 8) | far[way])
                def _():
                    zcopy(way, i - 3).wait_recv()

            @pl.when((s < 7) | ((s == 7) & far[way]))
            def _():
                zcopy(way, i).start()

        @pl.when(is_root)
        def _():
            for kind in range(2):
                @pl.when((i <= SPLIT) if kind == 0 else (i > SPLIT))
                def _():
                    for way in range(1 if own else 2):
                        if kind == 0:
                            for copy in root_copies(kind, way, i):
                                copy.start()
                        else:
                            @pl.when((s < 8) | far[way])
                            def _():
                                for copy in root_copies(kind, way, i):
                                    copy.start()

        if not own:
            @pl.when(sub == 2)
            def _():
                dcopy(slot_of(s, 0, c)).start()

                @pl.when(s < 8)
                def _():
                    dcopy(slot_of(s, 1, c)).start()

    def c_turn(kind, i):
        for tree in range(4):
            j = i - HOP * depths[kind][tree]
            if kind == 0:
                ok = (j >= 3 * (tree // 2)) & (j <= SPLIT)
            else:
                s, sub = piece(j)
                ok = (j > SPLIT) & ((s < 8) | ((j <= LAST) & far_part(tree // 2, sub, tree % 2)))

            @pl.when(ok)
            def _():
                ccopy(kind, tree, j, 0).wait_recv()

                def pass_on(n):
                    @pl.when(fans[kind][tree] > n)
                    def _():
                        ccopy(kind, tree, j, n).start()
                        if n + 1 < FAN:
                            pass_on(n + 1)

                pass_on(0)

    def drain(kind):
        def sent(tree, n, more):
            count = SPLIT + 1 - 3 * more if kind == 0 else 23 - SPLIT + more
            arrival(cols_buf.at[0:count], csend.at[kind, tree, n])

        @pl.when(is_root)
        def _():
            for way in range(2):
                for core in range(2):
                    @pl.when(c == core)
                    def _():
                        for n in range(2 * len(ROOT_FANS[kind])):
                            sent(2 * way + core, n, way if kind == 0 else 1 + (way == core))

        @pl.when(jnp.logical_not(is_root))
        def _():
            for tree in range(4):
                way, core = tree // 2, tree % 2
                for n in range(FAN):
                    @pl.when(fans[kind][tree] > n)
                    def _():
                        sent(tree, n, way if kind == 0 else 1 + (way == core))

    def drain_rows():
        arrival(rows_buf.at[0:45], zsend.at[0])
        arrival(rows_buf.at[0:48], dsend.at[0])

    def weights(j):
        lanes = pl.ds(pl.multiple_of(j * 128, 128), 128)

        def look(table, index):
            low, high = index & 127, index >> 7
            value = jnp.zeros((8, 128), jnp.float32)
            for r in range(16):
                row = jnp.broadcast_to(table[r:r + 1, :], (8, 128))
                value = jnp.where(high == r, jnp.take_along_axis(row, low, axis=1), value)
            return value

        @pl.when(j == 0)
        def _():
            for load in loads[6:]:
                load.wait()
            ibuf[...] = jnp.zeros_like(ibuf)
            ibuf[0, 0:3, :] = vi_ref[...]
            ibuf[1, 0:3, :] = ci_ref[...]

        w = 2.0 / (look(ve_ref, ibuf[0, :, lanes]) - look(ce_ref, ibuf[1, :, lanes]))
        for k in range(3):
            wcol[k, lanes, :] = jnp.broadcast_to(w[k:k + 1, :], (128, 128)).T

    def build(first, count):
        def fill(load):
            @pl.loop(0, count)
            def _(n):
                q = first + n
                s, way, core = (q + 2) // 4, ((q + 2) % 4) // 2, q % 2
                chip = (z + jnp.where(way == 1, s, DEEP - s)) % DEEP
                band = pl.multiple_of((2 * chip + core) * 16, 16)
                base = n * 96
                for k in range(3):
                    w = wcol[k, pl.ds(band, 16), :]
                    w = jnp.concatenate([w] * 4, axis=1)
                    re = (load(q, k, 0).astype(jnp.float32) * w).astype(jnp.bfloat16)
                    im = (load(q, k, 16).astype(jnp.float32) * w).astype(jnp.bfloat16)
                    top = pl.ds(pl.multiple_of(base + 32 * k, 16), 16)
                    low = pl.ds(pl.multiple_of(base + 32 * k + 16, 16), 16)
                    rhs[top, 0:512] = re
                    rhs[low, 0:512] = im
                    rhs[top, 512:1024] = -im
                    rhs[low, 512:1024] = re

        arrival(rows_buf.at[0:3 * count // 2], drecv.at[(first + 2) >> 3])

        @pl.when(is_root)
        def _():
            fill(lambda q, k, r: rows_buf[3 * q + k, c, r:r + 16, :])

        @pl.when(jnp.logical_not(is_root))
        def _():
            fill(lambda q, k, r: cols_buf[3 * q + k, r:r + 16, :])

    def block(first, count, r, fresh):
        at = pl.ds(pl.multiple_of(r * ROWS, ROWS), ROWS)
        left = rows_buf[3 * first:3 * (first + count), r].reshape(count * 96, ROWS)
        value = lax.dot_general(left, rhs[0:count * 96, :], (((0,), (0,)), ((), ())),
                                preferred_element_type=jnp.float32)
        for part in range(2):
            if fresh:
                out_ref[part, at, :] = value[:, part * 512:(part + 1) * 512]
            else:
                out_ref[part, at, :] += value[:, part * 512:(part + 1) * 512]

    blocks = 1024 // ROWS
    groups = [(0, 6), (6, 8), (14, 8), (22, 8), (30, 2)]
    depth0, depth1 = HOP * DEEPEST[0], HOP * DEEPEST[1]

    def ready(last_s):
        i = 3 * last_s + 2
        return i + depth0 if i <= SPLIT else max(SPLIT + depth0, i + depth1)

    begins = [ready(s) for s in (1, 3, 5, 7)]
    turns = LAST + depth1 + 1

    find_roles()
    arrival(rows_buf.at[pl.ds(3 * c, 3)], isem.at[0])
    pl.semaphore_wait(barrier, len(others))
    for i in range(3):
        z_turn(jnp.int32(i), own=True)
    dcopy(c).start()

    @pl.loop(0, turns)
    def _(i):
        @pl.when((i > 2) & (i <= LAST))
        def _():
            z_turn(i)

        @pl.when(jnp.logical_not(is_root))
        def _():
            @pl.when(i <= SPLIT + depth0)
            def _():
                c_turn(0, i)

            @pl.when(i > SPLIT)
            def _():
                c_turn(1, i)

        @pl.when((i >= 4) & (i < 8))
        def _():
            weights(i - 4)

        for n, begin in enumerate(begins):
            first, count = groups[n]

            @pl.when((i >= begin) & (i < begin + blocks))
            def _():
                @pl.when(i == begin)
                def _():
                    build(first, count)

                block(first, count, i - begin, n == 0)

    first, count = groups[4]
    build(first, count)

    @pl.loop(0, blocks)
    def _(r):
        block(first, count, r, False)

    drain(0)
    drain(1)
    drain_rows()


def shards(pair_matrix, valence_index, conduction_index, valence_energy, conduction_energy):
    x = jnp.swapaxes(pair_matrix, 2, 3).reshape(96, 1024)
    return pl.pallas_call(
        kernel,
        out_shape=jax.ShapeDtypeStruct((2, 1024, 512), jnp.float32),
        in_specs=[pl.BlockSpec(memory_space=pltpu.HBM)] * 5,
        out_specs=pl.BlockSpec(memory_space=pltpu.VMEM),
        scratch_shapes=[
            pltpu.VMEM((96, 2, SUB, 512), jnp.bfloat16),
            pltpu.VMEM((96, SUB, 512), jnp.bfloat16),
            pltpu.VMEM((768, 1024), jnp.bfloat16),
            pltpu.VMEM((3, 512, 128), jnp.float32),
            pltpu.VMEM((3, 512), jnp.int32),
            pltpu.VMEM((3, 512), jnp.int32),
            pltpu.VMEM((16, 128), jnp.float32),
            pltpu.VMEM((16, 128), jnp.float32),
            pltpu.VMEM((2, 8, 512), jnp.int32),
            pltpu.SemaphoreType.DMA((5,)),
            pltpu.SemaphoreType.DMA((1,)),
            pltpu.SemaphoreType.DMA((2, LAST - 2)),
            pltpu.SemaphoreType.DMA((1,)),
            pltpu.SemaphoreType.DMA((5,)),
            pltpu.SemaphoreType.DMA((2, 4, 4)),
            pltpu.SemaphoreType.DMA((4, LAST + 1)),
        ],
        compiler_params=pltpu.CompilerParams(collective_id=0, has_side_effects=True, vmem_limit_bytes=40 << 20),
        cost_estimate=pl.CostEstimate(flops=6 << 30, bytes_accessed=4 << 20, transcendentals=0),
        name="chi",
    )(x, valence_index, conduction_index, valence_energy.reshape(16, 128), conduction_energy.reshape(16, 128))


def solution(mesh):
    in_specs = (P(None, None, "grow", "gcol"), P(), P(), P(), P())
    out_specs = P(None, "grow", "gcol")
    return jax.shard_map(shards, mesh=mesh, in_specs=in_specs, out_specs=out_specs, check_vma=False)
```

```python
import functools

import jax
import jax.numpy as jnp
from jax import lax
from jax.experimental import pallas as pl
from jax.experimental.pallas import tpu as pltpu
from jax.sharding import PartitionSpec as P

MESH = pl.DeviceIdType.MESH
SIDE = 4
DEEP = 16
SUB = 32
LAST = 26
HOP = 3
ROWS = 512

TREES = [
    {
        (1, 0): (0, 1), (1, 3): (1, 0), (2, 3): (0, 3), (2, 1): (0, 3), (0, 1): (0, 3), (1, 2): (0, 3),
        (0, 3): (0, 3), (3, 3): (3, 0), (3, 0): (0, 1), (2, 2): (3, 0), (3, 2): (0, 3), (1, 1): (0, 3),
        (0, 2): (3, 0), (2, 0): (3, 0), (3, 1): (0, 3),
    },
    {
        (1, 0): (1, 0), (3, 0): (3, 0), (2, 0): (1, 0), (1, 2): (0, 2), (3, 1): (0, 1), (3, 3): (0, 3),
        (1, 1): (0, 3), (1, 3): (0, 1), (2, 3): (0, 3), (3, 2): (0, 1), (2, 1): (3, 0), (0, 3): (1, 0),
        (0, 1): (1, 0), (0, 2): (3, 0), (2, 2): (1, 0),
    },
]
SPLIT = 14
STEPS = [(1, 0), (3, 0), (0, 1), (0, 3), (0, 2), (2, 0)]


def children_of(tree, node):
    return [s for s in STEPS if tree.get(((node[0] + s[0]) % SIDE, (node[1] + s[1]) % SIDE)) == s]


def node_depth(tree, node):
    depth = 0
    while node != (0, 0):
        step = tree[node]
        node = ((node[0] - step[0]) % SIDE, (node[1] - step[1]) % SIDE)
        depth += 1
    return depth


NODES = [(px, py) for px in range(SIDE) for py in range(SIDE)]
ROOT_FANS = [children_of(t, (0, 0)) for t in TREES]
FAN = max(len(children_of(t, n)) for t in TREES for n in NODES if n != (0, 0))
DEEPEST = [max(node_depth(t, n) for n in NODES) for t in TREES]


def pick(place, values):
    shift = max(max(values).bit_length(), 1)
    per = 31 // shift
    result = jnp.int32(0)
    for start in range(0, len(values), per):
        part = values[start:start + per]
        word = sum(v << (shift * n) for n, v in enumerate(part))
        if word:
            here = (place >= start) & (place < start + per)
            offset = jnp.where(here, place - start, 0) * shift
            result = result + jnp.where(here, (word >> offset) & ((1 << shift) - 1), 0)
    return result


def turn(step, times):
    for _ in range(times):
        step = ((-step[1]) % SIDE, step[0] % SIDE)
    return step


def piece(i):
    s = (i * 11) >> 5
    return s, i - 3 * s


def slot_of(s, way, core):
    if way == 0:
        return jnp.where(s == 0, core, 4 * s - 2 + core)
    return jnp.where(s == 0, core, jnp.where(s == 8, 30 + core, 4 * s + core))


def far_part(way, sub, core):
    return (sub == 2 * way) | ((sub == 1) & (core == way))


def kernel(x_hbm, index_hbm, energy_hbm, out_ref, rows_buf, cols_buf, rhs, wcol, index_ref, energy_ref, ibuf,
           isem, zsend, zrecv, dsend, drecv, csend, crecv):
    g = lax.axis_index("grow")
    gc = lax.axis_index("gcol")
    x, y, z, c = g // SIDE, g % SIDE, gc // 2, gc % 2
    dx, dy = (x - z // SIDE + SIDE) % SIDE, (y - z % SIDE + SIDE) % SIDE
    is_root = (dx == 0) & (dy == 0)

    parts = [(x_hbm.at[SUB * k:SUB * (k + 1), 512 * h:512 * (h + 1)], rows_buf.at[3 * c + k, h])
             for k in range(3) for h in range(2)]
    parts += [(index_hbm, index_ref), (energy_hbm, energy_ref)]
    loads = [pltpu.make_async_copy(src, dst, isem.at[max(n - 5, 0)]) for n, (src, dst) in enumerate(parts)]
    for load in loads:
        load.start()

    def grow_at(step):
        return ((x + step[0]) % SIDE) * SIDE + (y + step[1]) % SIDE

    def dev(grow, gcol):
        return {"grow": grow, "gcol": gcol}

    ends = [((z + 1) % DEEP) * 2 + c, ((z + DEEP - 1) % DEEP) * 2 + c]
    sibling = dev(g, z * 2 + 1 - c)

    barrier = pltpu.get_barrier_semaphore()
    others = [dev(g, ends[0]), dev(g, ends[1]), sibling]
    others += [dev(grow_at(s), z * 2 + k) for s in STEPS for k in range(2)]
    for other in others:
        pl.semaphore_signal(barrier, inc=1, device_id=other, device_id_type=MESH)

    depths, fans, kids = [[], []], [[], []], [[], []]

    def find_roles():
        px, py = dx, dy
        for tree in range(4):
            place = px * SIDE + py
            for kind, table in enumerate(TREES):
                depths[kind].append(pick(place, [node_depth(table, n) for n in NODES]))
                lists = [children_of(table, n) if n != (0, 0) else [] for n in NODES]
                fans[kind].append(pick(place, [len(v) for v in lists]))
                mine = []
                for n in range(FAN):
                    codes = [STEPS.index(v[n]) if n < len(v) else 0 for v in lists]
                    code = pick(place, codes)
                    chip = jnp.int32(0)
                    for k in sorted(set(codes)):
                        chip = jnp.where(code == k, grow_at(turn(STEPS[k], tree)), chip)
                    mine.append(chip)
                kids[kind].append(mine)
            px, py = py, (SIDE - px) % SIDE

    def arrival(ref, sem):
        pltpu.make_async_copy(ref, ref, sem).wait()

    def zcopy(way, i):
        s, sub = piece(i)
        return pltpu.make_async_remote_copy(
            src_ref=rows_buf.at[3 * slot_of(s, way, c) + sub],
            dst_ref=rows_buf.at[3 * slot_of(s + 1, way, c) + sub],
            send_sem=zsend.at[0], recv_sem=zrecv.at[way, i],
            device_id=dev(g, ends[way]), device_id_type=MESH)

    def dcopy(slot):
        return pltpu.make_async_remote_copy(
            src_ref=rows_buf.at[pl.ds(3 * slot, 3)], dst_ref=rows_buf.at[pl.ds(3 * slot, 3)],
            send_sem=dsend.at[0], recv_sem=drecv.at[(slot + 2) >> 3],
            device_id=sibling, device_id_type=MESH)

    def root_copies(kind, way, i):
        s, sub = piece(i)
        slot = slot_of(s, way, c)
        tree = 2 * way + c
        copies = []
        for n, step in enumerate(ROOT_FANS[kind]):
            chip = jnp.where(c == 0, grow_at(turn(step, 2 * way)), grow_at(turn(step, 2 * way + 1)))
            for half in range(2):
                copies.append(pltpu.make_async_remote_copy(
                    src_ref=rows_buf.at[3 * slot + sub, half],
                    dst_ref=cols_buf.at[3 * slot + sub],
                    send_sem=csend.at[kind, tree, 2 * n + half], recv_sem=crecv.at[tree, i],
                    device_id=dev(chip, z * 2 + half), device_id_type=MESH))
        return copies

    def ccopy(kind, tree, i, n):
        s, sub = piece(i)
        slot = slot_of(s, tree // 2, tree % 2)
        return pltpu.make_async_remote_copy(
            src_ref=cols_buf.at[3 * slot + sub], dst_ref=cols_buf.at[3 * slot + sub],
            send_sem=csend.at[kind, tree, n], recv_sem=crecv.at[tree, i],
            device_id=dev(kids[kind][tree][n], gc), device_id_type=MESH)

    def z_turn(i, own=False):
        s, sub = piece(i)
        far = [far_part(way, sub, c) for way in range(2)]
        for way in range(2):
            if not own:
                @pl.when((s < 8) | far[way])
                def _():
                    zcopy(way, i - 3).wait_recv()

            @pl.when((s < 7) | ((s == 7) & far[way]))
            def _():
                zcopy(way, i).start()

        @pl.when(is_root)
        def _():
            for kind in range(2):
                @pl.when((i <= SPLIT) if kind == 0 else (i > SPLIT))
                def _():
                    for way in range(1 if own else 2):
                        if kind == 0:
                            for copy in root_copies(kind, way, i):
                                copy.start()
                        else:
                            @pl.when((s < 8) | far[way])
                            def _():
                                for copy in root_copies(kind, way, i):
                                    copy.start()

        if not own:
            @pl.when(sub == 2)
            def _():
                dcopy(slot_of(s, 0, c)).start()

                @pl.when(s < 8)
                def _():
                    dcopy(slot_of(s, 1, c)).start()

    def c_turn(kind, i):
        for tree in range(4):
            j = i - HOP * depths[kind][tree]
            if kind == 0:
                ok = (j >= 3 * (tree // 2)) & (j <= SPLIT)
            else:
                s, sub = piece(j)
                ok = (j > SPLIT) & ((s < 8) | ((j <= LAST) & far_part(tree // 2, sub, tree % 2)))

            @pl.when(ok)
            def _():
                ccopy(kind, tree, j, 0).wait_recv()

                def pass_on(n):
                    @pl.when(fans[kind][tree] > n)
                    def _():
                        ccopy(kind, tree, j, n).start()
                        if n + 1 < FAN:
                            pass_on(n + 1)

                pass_on(0)

    def drain(kind):
        def sent(tree, n, more):
            count = SPLIT + 1 - 3 * more if kind == 0 else 23 - SPLIT + more
            arrival(cols_buf.at[0:count], csend.at[kind, tree, n])

        @pl.when(is_root)
        def _():
            for way in range(2):
                for core in range(2):
                    @pl.when(c == core)
                    def _():
                        for n in range(2 * len(ROOT_FANS[kind])):
                            sent(2 * way + core, n, way if kind == 0 else 1 + (way == core))

        @pl.when(jnp.logical_not(is_root))
        def _():
            for tree in range(4):
                way, core = tree // 2, tree % 2
                for n in range(FAN):
                    @pl.when(fans[kind][tree] > n)
                    def _():
                        sent(tree, n, way if kind == 0 else 1 + (way == core))

    def drain_rows():
        arrival(rows_buf.at[0:45], zsend.at[0])
        arrival(rows_buf.at[0:48], dsend.at[0])

    def weights(j):
        lanes = pl.ds(pl.multiple_of(j * 128, 128), 128)

        def look(first, index):
            low, high = index & 127, index >> 7
            value = jnp.zeros((8, 128), jnp.float32)
            for r in range(16):
                row = jnp.broadcast_to(energy_ref[first + r:first + r + 1, :], (8, 128))
                value = jnp.where(high == r, jnp.take_along_axis(row, low, axis=1), value)
            return value

        @pl.when(j == 0)
        def _():
            for load in loads[6:]:
                load.wait()
            ibuf[...] = jnp.zeros_like(ibuf)
            ibuf[0, 0:3, :] = index_ref[0:3, :]
            ibuf[1, 0:3, :] = index_ref[3:6, :]

        w = 2.0 / (look(0, ibuf[0, :, lanes]) - look(16, ibuf[1, :, lanes]))
        for k in range(3):
            wcol[k, lanes, :] = jnp.broadcast_to(w[k:k + 1, :], (128, 128)).T

    def build(first, count):
        def fill(load):
            @pl.loop(0, count)
            def _(n):
                q = first + n
                s, way, core = (q + 2) // 4, ((q + 2) % 4) // 2, q % 2
                chip = (z + jnp.where(way == 1, s, DEEP - s)) % DEEP
                band = pl.multiple_of((2 * chip + core) * 16, 16)
                base = n * 96
                for k in range(3):
                    w = wcol[k, pl.ds(band, 16), :]
                    w = jnp.concatenate([w] * 4, axis=1)
                    re = (load(q, k, 0).astype(jnp.float32) * w).astype(jnp.bfloat16)
                    im = (load(q, k, 16).astype(jnp.float32) * w).astype(jnp.bfloat16)
                    top = pl.ds(pl.multiple_of(base + 32 * k, 16), 16)
                    low = pl.ds(pl.multiple_of(base + 32 * k + 16, 16), 16)
                    rhs[top, 0:512] = re
                    rhs[low, 0:512] = im
                    rhs[top, 512:1024] = -im
                    rhs[low, 512:1024] = re

        arrival(rows_buf.at[0:3 * count // 2], drecv.at[(first + 2) >> 3])

        @pl.when(is_root)
        def _():
            fill(lambda q, k, r: rows_buf[3 * q + k, c, r:r + 16, :])

        @pl.when(jnp.logical_not(is_root))
        def _():
            fill(lambda q, k, r: cols_buf[3 * q + k, r:r + 16, :])

    def block(first, count, r, fresh):
        at = pl.ds(pl.multiple_of(r * ROWS, ROWS), ROWS)
        left = rows_buf[3 * first:3 * (first + count), r].reshape(count * 96, ROWS)
        value = lax.dot_general(left, rhs[0:count * 96, :], (((0,), (0,)), ((), ())),
                                preferred_element_type=jnp.float32)
        for part in range(2):
            if fresh:
                out_ref[part, at, :] = value[:, part * 512:(part + 1) * 512]
            else:
                out_ref[part, at, :] += value[:, part * 512:(part + 1) * 512]

    blocks = 1024 // ROWS
    groups = [(0, 6), (6, 8), (14, 8), (22, 8), (30, 2)]
    depth0, depth1 = HOP * DEEPEST[0], HOP * DEEPEST[1]

    def ready(last_s):
        i = 3 * last_s + 2
        return i + depth0 if i <= SPLIT else max(SPLIT + depth0, i + depth1)

    begins = [ready(s) for s in (1, 3, 5, 7)]
    turns = LAST + depth1 + 1

    find_roles()
    arrival(rows_buf.at[pl.ds(3 * c, 3)], isem.at[0])
    pl.semaphore_wait(barrier, len(others))
    for i in range(3):
        z_turn(jnp.int32(i), own=True)
    dcopy(c).start()

    @pl.loop(0, turns)
    def _(i):
        @pl.when((i > 2) & (i <= LAST))
        def _():
            z_turn(i)

        @pl.when(jnp.logical_not(is_root))
        def _():
            @pl.when(i <= SPLIT + depth0)
            def _():
                c_turn(0, i)

            @pl.when(i > SPLIT)
            def _():
                c_turn(1, i)

        @pl.when((i >= 4) & (i < 8))
        def _():
            weights(i - 4)

        for n, begin in enumerate(begins):
            first, count = groups[n]

            @pl.when((i >= begin) & (i < begin + blocks))
            def _():
                @pl.when(i == begin)
                def _():
                    build(first, count)

                block(first, count, i - begin, n == 0)

    first, count = groups[4]
    build(first, count)

    @pl.loop(0, blocks)
    def _(r):
        block(first, count, r, False)

    drain(0)
    drain(1)
    drain_rows()


def shards(pair_matrix, valence_index, conduction_index, valence_energy, conduction_energy):
    x = jnp.swapaxes(pair_matrix, 2, 3).reshape(96, 1024)
    index = jnp.concatenate([valence_index, conduction_index])
    energy = jnp.concatenate([valence_energy, conduction_energy]).reshape(32, 128)
    return pl.pallas_call(
        kernel,
        out_shape=jax.ShapeDtypeStruct((2, 1024, 512), jnp.float32),
        in_specs=[pl.BlockSpec(memory_space=pltpu.HBM)] * 3,
        out_specs=pl.BlockSpec(memory_space=pltpu.VMEM),
        scratch_shapes=[
            pltpu.VMEM((96, 2, SUB, 512), jnp.bfloat16),
            pltpu.VMEM((96, SUB, 512), jnp.bfloat16),
            pltpu.VMEM((768, 1024), jnp.bfloat16),
            pltpu.VMEM((3, 512, 128), jnp.float32),
            pltpu.VMEM((6, 512), jnp.int32),
            pltpu.VMEM((32, 128), jnp.float32),
            pltpu.VMEM((2, 8, 512), jnp.int32),
            pltpu.SemaphoreType.DMA((3,)),
            pltpu.SemaphoreType.DMA((1,)),
            pltpu.SemaphoreType.DMA((2, LAST - 2)),
            pltpu.SemaphoreType.DMA((1,)),
            pltpu.SemaphoreType.DMA((5,)),
            pltpu.SemaphoreType.DMA((2, 4, 4)),
            pltpu.SemaphoreType.DMA((4, LAST + 1)),
        ],
        compiler_params=pltpu.CompilerParams(collective_id=0, has_side_effects=True, vmem_limit_bytes=40 << 20),
        cost_estimate=pl.CostEstimate(flops=6 << 30, bytes_accessed=4 << 20, transcendentals=0),
        name="chi",
    )(x, index, energy)


def solution(mesh):
    in_specs = (P(None, None, "grow", "gcol"), P(), P(), P(), P())
    out_specs = P(None, "grow", "gcol")
    return jax.shard_map(shards, mesh=mesh, in_specs=in_specs, out_specs=out_specs, check_vma=False)
```

```python
import functools

import jax
import jax.numpy as jnp
from jax import lax
from jax.experimental import pallas as pl
from jax.experimental.pallas import tpu as pltpu
from jax.sharding import PartitionSpec as P

MESH = pl.DeviceIdType.MESH
SIDE = 4
DEEP = 16
SUB = 32
LAST = 26
LAGS = [[0, 3, 6, 9, 12, 15], [0, 3, 6, 12]]
ROWS = 512

TREES = [
    {
        (1, 0): (0, 1), (1, 3): (1, 0), (2, 3): (0, 3), (2, 1): (0, 3), (0, 1): (0, 3), (1, 2): (0, 3),
        (0, 3): (0, 3), (3, 3): (3, 0), (3, 0): (0, 1), (2, 2): (3, 0), (3, 2): (0, 3), (1, 1): (0, 3),
        (0, 2): (3, 0), (2, 0): (3, 0), (3, 1): (0, 3),
    },
    {
        (1, 0): (1, 0), (3, 0): (3, 0), (2, 0): (1, 0), (1, 2): (0, 2), (3, 1): (0, 1), (3, 3): (0, 3),
        (1, 1): (0, 3), (1, 3): (0, 1), (2, 3): (0, 3), (3, 2): (0, 1), (2, 1): (3, 0), (0, 3): (1, 0),
        (0, 1): (1, 0), (0, 2): (3, 0), (2, 2): (1, 0),
    },
]
SPLIT = 14
STEPS = [(1, 0), (3, 0), (0, 1), (0, 3), (0, 2), (2, 0)]


def children_of(tree, node):
    return [s for s in STEPS if tree.get(((node[0] + s[0]) % SIDE, (node[1] + s[1]) % SIDE)) == s]


def node_depth(tree, node):
    depth = 0
    while node != (0, 0):
        step = tree[node]
        node = ((node[0] - step[0]) % SIDE, (node[1] - step[1]) % SIDE)
        depth += 1
    return depth


NODES = [(px, py) for px in range(SIDE) for py in range(SIDE)]
ROOT_FANS = [children_of(t, (0, 0)) for t in TREES]
FAN = max(len(children_of(t, n)) for t in TREES for n in NODES if n != (0, 0))


def pick(place, values):
    shift = max(max(values).bit_length(), 1)
    per = 31 // shift
    result = jnp.int32(0)
    for start in range(0, len(values), per):
        part = values[start:start + per]
        word = sum(v << (shift * n) for n, v in enumerate(part))
        if word:
            here = (place >= start) & (place < start + per)
            offset = jnp.where(here, place - start, 0) * shift
            result = result + jnp.where(here, (word >> offset) & ((1 << shift) - 1), 0)
    return result


def turn(step, times):
    for _ in range(times):
        step = ((-step[1]) % SIDE, step[0] % SIDE)
    return step


def piece(i):
    s = (i * 11) >> 5
    return s, i - 3 * s


def slot_of(s, way, core):
    if way == 0:
        return jnp.where(s == 0, core, 4 * s - 2 + core)
    return jnp.where(s == 0, core, jnp.where(s == 8, 30 + core, 4 * s + core))


def far_part(way, sub, core):
    return (sub == 2 * way) | ((sub == 1) & (core == way))


def kernel(x_hbm, index_hbm, energy_hbm, out_ref, rows_buf, cols_buf, rhs, wcol, index_ref, energy_ref, ibuf,
           isem, zsend, zrecv, dsend, drecv, csend, crecv):
    g = lax.axis_index("grow")
    gc = lax.axis_index("gcol")
    x, y, z, c = g // SIDE, g % SIDE, gc // 2, gc % 2
    dx, dy = (x - z // SIDE + SIDE) % SIDE, (y - z % SIDE + SIDE) % SIDE
    is_root = (dx == 0) & (dy == 0)

    parts = [(x_hbm.at[SUB * k:SUB * (k + 1), 512 * h:512 * (h + 1)], rows_buf.at[3 * c + k, h])
             for k in range(3) for h in range(2)]
    parts += [(index_hbm, index_ref), (energy_hbm, energy_ref)]
    loads = [pltpu.make_async_copy(src, dst, isem.at[max(n - 5, 0)]) for n, (src, dst) in enumerate(parts)]
    for load in loads[:6]:
        load.start()

    def grow_at(step):
        return ((x + step[0]) % SIDE) * SIDE + (y + step[1]) % SIDE

    def dev(grow, gcol):
        return {"grow": grow, "gcol": gcol}

    ends = [((z + 1) % DEEP) * 2 + c, ((z + DEEP - 1) % DEEP) * 2 + c]
    sibling = dev(g, z * 2 + 1 - c)

    barrier = pltpu.get_barrier_semaphore()
    others = [dev(g, ends[0]), dev(g, ends[1]), sibling]
    others += [dev(grow_at(s), z * 2 + k) for s in STEPS for k in range(2)]
    for other in others:
        pl.semaphore_signal(barrier, inc=1, device_id=other, device_id_type=MESH)
    for load in loads[6:]:
        load.start()

    lags, fans, kids = [[], []], [[], []], [[], []]

    def find_roles():
        px, py = dx, dy
        for tree in range(4):
            place = px * SIDE + py
            for kind, table in enumerate(TREES):
                lags[kind].append(pick(place, [LAGS[kind][node_depth(table, n)] for n in NODES]))
                lists = [children_of(table, n) if n != (0, 0) else [] for n in NODES]
                fans[kind].append(pick(place, [len(v) for v in lists]))
                mine = []
                for n in range(FAN):
                    codes = [STEPS.index(v[n]) if n < len(v) else 0 for v in lists]
                    code = pick(place, codes)
                    chip = jnp.int32(0)
                    for k in sorted(set(codes)):
                        chip = jnp.where(code == k, grow_at(turn(STEPS[k], tree)), chip)
                    mine.append(chip)
                kids[kind].append(mine)
            px, py = py, (SIDE - px) % SIDE

    def arrival(ref, sem):
        pltpu.make_async_copy(ref, ref, sem).wait()

    def zcopy(way, i):
        s, sub = piece(i)
        return pltpu.make_async_remote_copy(
            src_ref=rows_buf.at[3 * slot_of(s, way, c) + sub],
            dst_ref=rows_buf.at[3 * slot_of(s + 1, way, c) + sub],
            send_sem=zsend.at[0], recv_sem=zrecv.at[way, i],
            device_id=dev(g, ends[way]), device_id_type=MESH)

    def dcopy(slot, sub):
        return pltpu.make_async_remote_copy(
            src_ref=rows_buf.at[3 * slot + sub], dst_ref=rows_buf.at[3 * slot + sub],
            send_sem=dsend.at[0], recv_sem=drecv.at[(slot + 2) >> 3],
            device_id=sibling, device_id_type=MESH)

    def root_copies(kind, way, i):
        s, sub = piece(i)
        slot = slot_of(s, way, c)
        tree = 2 * way + c
        copies = []
        for n, step in enumerate(ROOT_FANS[kind]):
            chip = jnp.where(c == 0, grow_at(turn(step, 2 * way)), grow_at(turn(step, 2 * way + 1)))
            for half in range(2):
                copies.append(pltpu.make_async_remote_copy(
                    src_ref=rows_buf.at[3 * slot + sub, half],
                    dst_ref=cols_buf.at[3 * slot + sub],
                    send_sem=csend.at[kind, tree, 2 * n + half], recv_sem=crecv.at[tree, i],
                    device_id=dev(chip, z * 2 + half), device_id_type=MESH))
        return copies

    def ccopy(kind, tree, i, n):
        s, sub = piece(i)
        slot = slot_of(s, tree // 2, tree % 2)
        return pltpu.make_async_remote_copy(
            src_ref=cols_buf.at[3 * slot + sub], dst_ref=cols_buf.at[3 * slot + sub],
            send_sem=csend.at[kind, tree, n], recv_sem=crecv.at[tree, i],
            device_id=dev(kids[kind][tree][n], gc), device_id_type=MESH)

    def z_turn(i, own=False):
        s, sub = piece(i)
        far = [far_part(way, sub, c) for way in range(2)]
        for way in range(2):
            if not own:
                @pl.when((s < 8) | far[way])
                def _():
                    zcopy(way, i - 3).wait_recv()

            @pl.when((s < 7) | ((s == 7) & far[way]))
            def _():
                zcopy(way, i).start()

        @pl.when(is_root)
        def _():
            for kind in range(2):
                @pl.when((i <= SPLIT) if kind == 0 else (i > SPLIT))
                def _():
                    for way in range(1 if own else 2):
                        if kind == 0:
                            for copy in root_copies(kind, way, i):
                                copy.start()
                        else:
                            @pl.when((s < 8) | far[way])
                            def _():
                                for copy in root_copies(kind, way, i):
                                    copy.start()

        for way in range(1 if own else 2):
            @pl.when((s < 8) | far[way])
            def _():
                dcopy(slot_of(s, way, c), sub).start()

    def c_turn(kind, i):
        for tree in range(4):
            j = i - lags[kind][tree]
            if kind == 0:
                ok = (j >= 3 * (tree // 2)) & (j <= SPLIT)
            else:
                s, sub = piece(j)
                ok = (j > SPLIT) & ((s < 8) | ((j <= LAST) & far_part(tree // 2, sub, tree % 2)))

            @pl.when(ok)
            def _():
                ccopy(kind, tree, j, 0).wait_recv()

                def pass_on(n):
                    @pl.when(fans[kind][tree] > n)
                    def _():
                        ccopy(kind, tree, j, n).start()
                        if n + 1 < FAN:
                            pass_on(n + 1)

                pass_on(0)

    def drain(kind):
        def sent(tree, n, more):
            count = SPLIT + 1 - 3 * more if kind == 0 else 23 - SPLIT + more
            arrival(cols_buf.at[0:count], csend.at[kind, tree, n])

        @pl.when(is_root)
        def _():
            for way in range(2):
                for core in range(2):
                    @pl.when(c == core)
                    def _():
                        for n in range(2 * len(ROOT_FANS[kind])):
                            sent(2 * way + core, n, way if kind == 0 else 1 + (way == core))

        @pl.when(jnp.logical_not(is_root))
        def _():
            for tree in range(4):
                way, core = tree // 2, tree % 2
                for n in range(FAN):
                    @pl.when(fans[kind][tree] > n)
                    def _():
                        sent(tree, n, way if kind == 0 else 1 + (way == core))

    def drain_rows():
        arrival(rows_buf.at[0:45], zsend.at[0])
        arrival(rows_buf.at[0:48], dsend.at[0])

    def weights(j):
        lanes = pl.ds(pl.multiple_of(j * 128, 128), 128)

        def look(first, index):
            low, high = index & 127, index >> 7
            value = jnp.zeros((8, 128), jnp.float32)
            for r in range(16):
                row = jnp.broadcast_to(energy_ref[first + r:first + r + 1, :], (8, 128))
                value = jnp.where(high == r, jnp.take_along_axis(row, low, axis=1), value)
            return value

        @pl.when(j == 0)
        def _():
            for load in loads[6:]:
                load.wait()
            ibuf[...] = jnp.zeros_like(ibuf)
            ibuf[0, 0:3, :] = index_ref[0:3, :]
            ibuf[1, 0:3, :] = index_ref[3:6, :]

        w = 2.0 / (look(0, ibuf[0, :, lanes]) - look(16, ibuf[1, :, lanes]))
        for k in range(3):
            wcol[k, lanes, :] = jnp.broadcast_to(w[k:k + 1, :], (128, 128)).T

    def build(first, count):
        def fill(load):
            @pl.loop(0, count)
            def _(n):
                q = first + n
                s, way, core = (q + 2) // 4, ((q + 2) % 4) // 2, q % 2
                chip = (z + jnp.where(way == 1, s, DEEP - s)) % DEEP
                band = pl.multiple_of((2 * chip + core) * 16, 16)
                base = n * 96
                for k in range(3):
                    w = wcol[k, pl.ds(band, 16), :]
                    w = jnp.concatenate([w] * 4, axis=1)
                    re = (load(q, k, 0).astype(jnp.float32) * w).astype(jnp.bfloat16)
                    im = (load(q, k, 16).astype(jnp.float32) * w).astype(jnp.bfloat16)
                    top = pl.ds(pl.multiple_of(base + 32 * k, 16), 16)
                    low = pl.ds(pl.multiple_of(base + 32 * k + 16, 16), 16)
                    rhs[top, 0:512] = re
                    rhs[low, 0:512] = im
                    rhs[top, 512:1024] = -im
                    rhs[low, 512:1024] = re

        arrival(rows_buf.at[0:3 * count // 2], drecv.at[(first + 2) >> 3])

        @pl.when(is_root)
        def _():
            fill(lambda q, k, r: rows_buf[3 * q + k, c, r:r + 16, :])

        @pl.when(jnp.logical_not(is_root))
        def _():
            fill(lambda q, k, r: cols_buf[3 * q + k, r:r + 16, :])

    def block(first, count, r, fresh):
        at = pl.ds(pl.multiple_of(r * ROWS, ROWS), ROWS)
        left = rows_buf[3 * first:3 * (first + count), r].reshape(count * 96, ROWS)
        value = lax.dot_general(left, rhs[0:count * 96, :], (((0,), (0,)), ((), ())),
                                preferred_element_type=jnp.float32)
        for part in range(2):
            if fresh:
                out_ref[part, at, :] = value[:, part * 512:(part + 1) * 512]
            else:
                out_ref[part, at, :] += value[:, part * 512:(part + 1) * 512]

    blocks = 1024 // ROWS
    groups = [(0, 6), (6, 8), (14, 8), (22, 8), (30, 2)]
    depth0, depth1 = LAGS[0][-1], LAGS[1][-1]

    def ready(last_s):
        i = 3 * last_s + 2
        return i + depth0 if i <= SPLIT else max(SPLIT + depth0, i + depth1)

    begins = [ready(s) for s in (1, 3, 5, 7)]
    turns = LAST + depth1 + 1

    arrival(rows_buf.at[pl.ds(3 * c, 3)], isem.at[0])
    pl.semaphore_wait(barrier, len(others))
    for i in range(3):
        z_turn(jnp.int32(i), own=True)
    find_roles()

    @pl.loop(0, turns)
    def _(i):
        @pl.when((i > 2) & (i <= LAST))
        def _():
            z_turn(i)

        @pl.when(jnp.logical_not(is_root))
        def _():
            @pl.when(i <= SPLIT + depth0)
            def _():
                c_turn(0, i)

            @pl.when(i > SPLIT)
            def _():
                c_turn(1, i)

        @pl.when((i >= 4) & (i < 8))
        def _():
            weights(i - 4)

        for n, begin in enumerate(begins):
            first, count = groups[n]

            @pl.when((i >= begin) & (i < begin + blocks))
            def _():
                @pl.when(i == begin)
                def _():
                    build(first, count)

                block(first, count, i - begin, n == 0)

    drain(0)
    drain_rows()
    first, count = groups[4]
    build(first, count)

    @pl.loop(0, blocks)
    def _(r):
        block(first, count, r, False)

    drain(1)


def shards(pair_matrix, valence_index, conduction_index, valence_energy, conduction_energy):
    x = jnp.swapaxes(pair_matrix, 2, 3).reshape(96, 1024)
    index = jnp.concatenate([valence_index, conduction_index])
    energy = jnp.concatenate([valence_energy, conduction_energy]).reshape(32, 128)
    return pl.pallas_call(
        kernel,
        out_shape=jax.ShapeDtypeStruct((2, 1024, 512), jnp.float32),
        in_specs=[pl.BlockSpec(memory_space=pltpu.HBM)] * 3,
        out_specs=pl.BlockSpec(memory_space=pltpu.VMEM),
        scratch_shapes=[
            pltpu.VMEM((96, 2, SUB, 512), jnp.bfloat16),
            pltpu.VMEM((96, SUB, 512), jnp.bfloat16),
            pltpu.VMEM((768, 1024), jnp.bfloat16),
            pltpu.VMEM((3, 512, 128), jnp.float32),
            pltpu.VMEM((6, 512), jnp.int32),
            pltpu.VMEM((32, 128), jnp.float32),
            pltpu.VMEM((2, 8, 512), jnp.int32),
            pltpu.SemaphoreType.DMA((3,)),
            pltpu.SemaphoreType.DMA((1,)),
            pltpu.SemaphoreType.DMA((2, LAST - 2)),
            pltpu.SemaphoreType.DMA((1,)),
            pltpu.SemaphoreType.DMA((5,)),
            pltpu.SemaphoreType.DMA((2, 4, 4)),
            pltpu.SemaphoreType.DMA((4, LAST + 1)),
        ],
        compiler_params=pltpu.CompilerParams(collective_id=0, has_side_effects=True, vmem_limit_bytes=40 << 20),
        cost_estimate=pl.CostEstimate(flops=6 << 30, bytes_accessed=4 << 20, transcendentals=0),
        name="chi",
    )(x, index, energy)


def solution(mesh):
    in_specs = (P(None, None, "grow", "gcol"), P(), P(), P(), P())
    out_specs = P(None, "grow", "gcol")
    return jax.shard_map(shards, mesh=mesh, in_specs=in_specs, out_specs=out_specs, check_vma=False)
```

```python
import functools

import jax
import jax.numpy as jnp
from jax import lax
from jax.experimental import pallas as pl
from jax.experimental.pallas import tpu as pltpu
from jax.sharding import PartitionSpec as P

MESH = pl.DeviceIdType.MESH
SIDE = 4
DEEP = 16
SUB = 32
LAST = 26
LAGS = [[0, 3, 6, 9, 12, 15], [0, 3, 6, 12]]
ROWS = 512

TREES = [
    {
        (1, 0): (0, 1), (1, 3): (1, 0), (2, 3): (0, 3), (2, 1): (0, 3), (0, 1): (0, 3), (1, 2): (0, 3),
        (0, 3): (0, 3), (3, 3): (3, 0), (3, 0): (0, 1), (2, 2): (3, 0), (3, 2): (0, 3), (1, 1): (0, 3),
        (0, 2): (3, 0), (2, 0): (3, 0), (3, 1): (0, 3),
    },
    {
        (1, 0): (1, 0), (3, 0): (3, 0), (2, 0): (1, 0), (1, 2): (0, 2), (3, 1): (0, 1), (3, 3): (0, 3),
        (1, 1): (0, 3), (1, 3): (0, 1), (2, 3): (0, 3), (3, 2): (0, 1), (2, 1): (3, 0), (0, 3): (1, 0),
        (0, 1): (1, 0), (0, 2): (3, 0), (2, 2): (1, 0),
    },
]
SPLIT = 14
STEPS = [(1, 0), (3, 0), (0, 1), (0, 3), (0, 2), (2, 0)]


def children_of(tree, node):
    return [s for s in STEPS if tree.get(((node[0] + s[0]) % SIDE, (node[1] + s[1]) % SIDE)) == s]


def node_depth(tree, node):
    depth = 0
    while node != (0, 0):
        step = tree[node]
        node = ((node[0] - step[0]) % SIDE, (node[1] - step[1]) % SIDE)
        depth += 1
    return depth


NODES = [(px, py) for px in range(SIDE) for py in range(SIDE)]
ROOT_FANS = [children_of(t, (0, 0)) for t in TREES]
FAN = max(len(children_of(t, n)) for t in TREES for n in NODES if n != (0, 0))


def pick(place, values):
    shift = max(max(values).bit_length(), 1)
    per = 31 // shift
    result = jnp.int32(0)
    for start in range(0, len(values), per):
        part = values[start:start + per]
        word = sum(v << (shift * n) for n, v in enumerate(part))
        if word:
            here = (place >= start) & (place < start + per)
            offset = jnp.where(here, place - start, 0) * shift
            result = result + jnp.where(here, (word >> offset) & ((1 << shift) - 1), 0)
    return result


def turn(step, times):
    for _ in range(times):
        step = ((-step[1]) % SIDE, step[0] % SIDE)
    return step


def piece(i):
    s = (i * 11) >> 5
    return s, i - 3 * s


def slot_of(s, way, core):
    if way == 0:
        return jnp.where(s == 0, core, 4 * s - 2 + core)
    return jnp.where(s == 0, core, jnp.where(s == 8, 30 + core, 4 * s + core))


def far_part(way, sub, core):
    return (sub == 2 * way) | ((sub == 1) & (core == way))


def kernel(x_hbm, index_hbm, energy_hbm, out_ref, left_ref, rhs_ref, rows_buf, cols_buf, rhs, wcol, index_ref, energy_ref, ibuf,
           isem, zsend, zrecv, dsend, drecv, csend, crecv):
    g = lax.axis_index("grow")
    gc = lax.axis_index("gcol")
    x, y, z, c = g // SIDE, g % SIDE, gc // 2, gc % 2
    dx, dy = (x - z // SIDE + SIDE) % SIDE, (y - z % SIDE + SIDE) % SIDE
    is_root = (dx == 0) & (dy == 0)

    parts = [(x_hbm.at[SUB * k:SUB * (k + 1), 512 * h:512 * (h + 1)], rows_buf.at[3 * c + k, h])
             for k in range(3) for h in range(2)]
    parts += [(index_hbm, index_ref), (energy_hbm, energy_ref)]
    loads = [pltpu.make_async_copy(src, dst, isem.at[max(n - 5, 0)]) for n, (src, dst) in enumerate(parts)]
    for load in loads[:6]:
        load.start()

    def grow_at(step):
        return ((x + step[0]) % SIDE) * SIDE + (y + step[1]) % SIDE

    def dev(grow, gcol):
        return {"grow": grow, "gcol": gcol}

    ends = [((z + 1) % DEEP) * 2 + c, ((z + DEEP - 1) % DEEP) * 2 + c]
    sibling = dev(g, z * 2 + 1 - c)

    barrier = pltpu.get_barrier_semaphore()
    others = [dev(g, ends[0]), dev(g, ends[1]), sibling]
    others += [dev(grow_at(s), z * 2 + k) for s in STEPS for k in range(2)]
    for other in others:
        pl.semaphore_signal(barrier, inc=1, device_id=other, device_id_type=MESH)
    for load in loads[6:]:
        load.start()

    lags, fans, kids = [[], []], [[], []], [[], []]

    def find_roles():
        px, py = dx, dy
        for tree in range(4):
            place = px * SIDE + py
            for kind, table in enumerate(TREES):
                lags[kind].append(pick(place, [LAGS[kind][node_depth(table, n)] for n in NODES]))
                lists = [children_of(table, n) if n != (0, 0) else [] for n in NODES]
                fans[kind].append(pick(place, [len(v) for v in lists]))
                mine = []
                for n in range(FAN):
                    codes = [STEPS.index(v[n]) if n < len(v) else 0 for v in lists]
                    code = pick(place, codes)
                    chip = jnp.int32(0)
                    for k in sorted(set(codes)):
                        chip = jnp.where(code == k, grow_at(turn(STEPS[k], tree)), chip)
                    mine.append(chip)
                kids[kind].append(mine)
            px, py = py, (SIDE - px) % SIDE

    def arrival(ref, sem):
        pltpu.make_async_copy(ref, ref, sem).wait()

    def zcopy(way, i):
        s, sub = piece(i)
        return pltpu.make_async_remote_copy(
            src_ref=rows_buf.at[3 * slot_of(s, way, c) + sub],
            dst_ref=rows_buf.at[3 * slot_of(s + 1, way, c) + sub],
            send_sem=zsend.at[0], recv_sem=zrecv.at[way, i],
            device_id=dev(g, ends[way]), device_id_type=MESH)

    def dcopy(slot, sub):
        return pltpu.make_async_remote_copy(
            src_ref=rows_buf.at[3 * slot + sub], dst_ref=rows_buf.at[3 * slot + sub],
            send_sem=dsend.at[0], recv_sem=drecv.at[(slot + 2) >> 3],
            device_id=sibling, device_id_type=MESH)

    def root_copies(kind, way, i):
        s, sub = piece(i)
        slot = slot_of(s, way, c)
        tree = 2 * way + c
        copies = []
        for n, step in enumerate(ROOT_FANS[kind]):
            chip = jnp.where(c == 0, grow_at(turn(step, 2 * way)), grow_at(turn(step, 2 * way + 1)))
            for half in range(2):
                copies.append(pltpu.make_async_remote_copy(
                    src_ref=rows_buf.at[3 * slot + sub, half],
                    dst_ref=cols_buf.at[3 * slot + sub],
                    send_sem=csend.at[kind, tree, 2 * n + half], recv_sem=crecv.at[tree, i],
                    device_id=dev(chip, z * 2 + half), device_id_type=MESH))
        return copies

    def ccopy(kind, tree, i, n):
        s, sub = piece(i)
        slot = slot_of(s, tree // 2, tree % 2)
        return pltpu.make_async_remote_copy(
            src_ref=cols_buf.at[3 * slot + sub], dst_ref=cols_buf.at[3 * slot + sub],
            send_sem=csend.at[kind, tree, n], recv_sem=crecv.at[tree, i],
            device_id=dev(kids[kind][tree][n], gc), device_id_type=MESH)

    def z_turn(i, own=False):
        s, sub = piece(i)
        far = [far_part(way, sub, c) for way in range(2)]
        for way in range(2):
            if not own:
                @pl.when((s < 8) | far[way])
                def _():
                    zcopy(way, i - 3).wait_recv()

            @pl.when((s < 7) | ((s == 7) & far[way]))
            def _():
                zcopy(way, i).start()

        @pl.when(is_root)
        def _():
            for kind in range(2):
                @pl.when((i <= SPLIT) if kind == 0 else (i > SPLIT))
                def _():
                    for way in range(1 if own else 2):
                        if kind == 0:
                            for copy in root_copies(kind, way, i):
                                copy.start()
                        else:
                            @pl.when((s < 8) | far[way])
                            def _():
                                for copy in root_copies(kind, way, i):
                                    copy.start()

        for way in range(1 if own else 2):
            @pl.when((s < 8) | far[way])
            def _():
                dcopy(slot_of(s, way, c), sub).start()

    def c_turn(kind, i):
        for tree in range(4):
            j = i - lags[kind][tree]
            if kind == 0:
                ok = (j >= 3 * (tree // 2)) & (j <= SPLIT)
            else:
                s, sub = piece(j)
                ok = (j > SPLIT) & ((s < 8) | ((j <= LAST) & far_part(tree // 2, sub, tree % 2)))

            @pl.when(ok)
            def _():
                ccopy(kind, tree, j, 0).wait_recv()

                def pass_on(n):
                    @pl.when(fans[kind][tree] > n)
                    def _():
                        ccopy(kind, tree, j, n).start()
                        if n + 1 < FAN:
                            pass_on(n + 1)

                pass_on(0)

    def drain(kind):
        def sent(tree, n, more):
            count = SPLIT + 1 - 3 * more if kind == 0 else 23 - SPLIT + more
            arrival(cols_buf.at[0:count], csend.at[kind, tree, n])

        @pl.when(is_root)
        def _():
            for way in range(2):
                for core in range(2):
                    @pl.when(c == core)
                    def _():
                        for n in range(2 * len(ROOT_FANS[kind])):
                            sent(2 * way + core, n, way if kind == 0 else 1 + (way == core))

        @pl.when(jnp.logical_not(is_root))
        def _():
            for tree in range(4):
                way, core = tree // 2, tree % 2
                for n in range(FAN):
                    @pl.when(fans[kind][tree] > n)
                    def _():
                        sent(tree, n, way if kind == 0 else 1 + (way == core))

    def drain_rows():
        arrival(rows_buf.at[0:45], zsend.at[0])
        arrival(rows_buf.at[0:48], dsend.at[0])

    def weights(j):
        lanes = pl.ds(pl.multiple_of(j * 128, 128), 128)

        def look(first, index):
            low, high = index & 127, index >> 7
            value = jnp.zeros((8, 128), jnp.float32)
            for r in range(16):
                row = jnp.broadcast_to(energy_ref[first + r:first + r + 1, :], (8, 128))
                value = jnp.where(high == r, jnp.take_along_axis(row, low, axis=1), value)
            return value

        @pl.when(j == 0)
        def _():
            for load in loads[6:]:
                load.wait()
            ibuf[...] = jnp.zeros_like(ibuf)
            ibuf[0, 0:3, :] = index_ref[0:3, :]
            ibuf[1, 0:3, :] = index_ref[3:6, :]

        w = 2.0 / (look(0, ibuf[0, :, lanes]) - look(16, ibuf[1, :, lanes]))
        for k in range(3):
            wcol[k, lanes, :] = jnp.broadcast_to(w[k:k + 1, :], (128, 128)).T

    def build(first, count, rhs):
        def fill(load):
            @pl.loop(0, count)
            def _(n):
                q = first + n
                s, way, core = (q + 2) // 4, ((q + 2) % 4) // 2, q % 2
                chip = (z + jnp.where(way == 1, s, DEEP - s)) % DEEP
                band = pl.multiple_of((2 * chip + core) * 16, 16)
                base = n * 96
                for k in range(3):
                    w = wcol[k, pl.ds(band, 16), :]
                    w = jnp.concatenate([w] * 4, axis=1)
                    re = (load(q, k, 0).astype(jnp.float32) * w).astype(jnp.bfloat16)
                    im = (load(q, k, 16).astype(jnp.float32) * w).astype(jnp.bfloat16)
                    top = pl.ds(pl.multiple_of(base + 32 * k, 16), 16)
                    low = pl.ds(pl.multiple_of(base + 32 * k + 16, 16), 16)
                    rhs[top, 0:512] = re
                    rhs[low, 0:512] = im
                    rhs[top, 512:1024] = -im
                    rhs[low, 512:1024] = re

        arrival(rows_buf.at[0:3 * count // 2], drecv.at[(first + 2) >> 3])

        @pl.when(is_root)
        def _():
            fill(lambda q, k, r: rows_buf[3 * q + k, c, r:r + 16, :])

        @pl.when(jnp.logical_not(is_root))
        def _():
            fill(lambda q, k, r: cols_buf[3 * q + k, r:r + 16, :])

    def block(first, count, r, fresh):
        at = pl.ds(pl.multiple_of(r * ROWS, ROWS), ROWS)
        left = rows_buf[3 * first:3 * (first + count), r].reshape(count * 96, ROWS)
        value = lax.dot_general(left, rhs[0:count * 96, :], (((0,), (0,)), ((), ())),
                                preferred_element_type=jnp.float32)
        for part in range(2):
            if fresh:
                out_ref[part, at, :] = value[:, part * 512:(part + 1) * 512]
            else:
                out_ref[part, at, :] += value[:, part * 512:(part + 1) * 512]

    blocks = 1024 // ROWS
    groups = [(0, 6), (6, 8), (14, 8), (22, 8), (30, 2)]
    depth0, depth1 = LAGS[0][-1], LAGS[1][-1]

    def ready(last_s):
        i = 3 * last_s + 2
        return i + depth0 if i <= SPLIT else max(SPLIT + depth0, i + depth1)

    begins = [ready(s) for s in (1, 3, 5, 7)]
    turns = LAST + depth1 + 1

    arrival(rows_buf.at[pl.ds(3 * c, 3)], isem.at[0])
    pl.semaphore_wait(barrier, len(others))
    for i in range(3):
        z_turn(jnp.int32(i), own=True)
    find_roles()

    @pl.loop(0, turns)
    def _(i):
        @pl.when((i > 2) & (i <= LAST))
        def _():
            z_turn(i)

        @pl.when(jnp.logical_not(is_root))
        def _():
            @pl.when(i <= SPLIT + depth0)
            def _():
                c_turn(0, i)

            @pl.when(i > SPLIT)
            def _():
                c_turn(1, i)

        @pl.when((i >= 4) & (i < 8))
        def _():
            weights(i - 4)

        for n, begin in enumerate(begins):
            first, count = groups[n]

            @pl.when((i >= begin) & (i < begin + blocks))
            def _():
                @pl.when(i == begin)
                def _():
                    build(first, count, rhs)

                block(first, count, i - begin, n == 0)

    drain(0)
    drain_rows()
    first, count = groups[4]
    build(first, count, rhs_ref)
    left_ref[...] = rows_buf[3 * first:3 * (first + count)]
    drain(1)


def finish(sum_ref, left_ref, rhs_ref, out_ref, part_buf, osem):
    def write(r):
        at = pl.ds(pl.multiple_of(r * 256, 256), 256)
        return pltpu.make_async_copy(part_buf.at[:, at], out_ref.at[:, at], osem.at[r])

    for r in range(4):
        left = left_ref[:, r // 2, :, (r % 2) * 256:(r % 2 + 1) * 256].reshape(6 * SUB, 256)
        value = lax.dot_general(left, rhs_ref[...], (((0,), (0,)), ((), ())), preferred_element_type=jnp.float32)
        for part in range(2):
            at = slice(r * 256, (r + 1) * 256)
            part_buf[part, at, :] = sum_ref[part, at, :] + value[:, part * 512:(part + 1) * 512]
        write(r).start()
    for r in range(4):
        write(r).wait()


def shards(pair_matrix, valence_index, conduction_index, valence_energy, conduction_energy):
    x = jnp.swapaxes(pair_matrix, 2, 3).reshape(96, 1024)
    index = jnp.concatenate([valence_index, conduction_index])
    energy = jnp.concatenate([valence_energy, conduction_energy]).reshape(32, 128)
    total, left, right = pl.pallas_call(
        kernel,
        out_shape=[jax.ShapeDtypeStruct((2, 1024, 512), jnp.float32),
                   jax.ShapeDtypeStruct((6, 2, SUB, 512), jnp.bfloat16),
                   jax.ShapeDtypeStruct((6 * SUB, 1024), jnp.bfloat16)],
        in_specs=[pl.BlockSpec(memory_space=pltpu.HBM)] * 3,
        out_specs=[pl.BlockSpec(memory_space=pltpu.VMEM)] * 3,
        scratch_shapes=[
            pltpu.VMEM((96, 2, SUB, 512), jnp.bfloat16),
            pltpu.VMEM((96, SUB, 512), jnp.bfloat16),
            pltpu.VMEM((768, 1024), jnp.bfloat16),
            pltpu.VMEM((3, 512, 128), jnp.float32),
            pltpu.VMEM((6, 512), jnp.int32),
            pltpu.VMEM((32, 128), jnp.float32),
            pltpu.VMEM((2, 8, 512), jnp.int32),
            pltpu.SemaphoreType.DMA((3,)),
            pltpu.SemaphoreType.DMA((1,)),
            pltpu.SemaphoreType.DMA((2, LAST - 2)),
            pltpu.SemaphoreType.DMA((1,)),
            pltpu.SemaphoreType.DMA((5,)),
            pltpu.SemaphoreType.DMA((2, 4, 4)),
            pltpu.SemaphoreType.DMA((4, LAST + 1)),
        ],
        compiler_params=pltpu.CompilerParams(collective_id=0, has_side_effects=True, vmem_limit_bytes=32 << 20),
        cost_estimate=pl.CostEstimate(flops=6 << 30, bytes_accessed=4 << 20, transcendentals=0),
        name="chi",
    )(x, index, energy)
    return pl.pallas_call(
        finish,
        out_shape=jax.ShapeDtypeStruct((2, 1024, 512), jnp.float32),
        in_specs=[pl.BlockSpec(memory_space=pltpu.VMEM)] * 3,
        out_specs=pl.BlockSpec(memory_space=pl.ANY),
        scratch_shapes=[pltpu.VMEM((2, 1024, 512), jnp.float32), pltpu.SemaphoreType.DMA((4,))],
        compiler_params=pltpu.CompilerParams(vmem_limit_bytes=16 << 20),
        name="finish",
    )(total, left, right)


def solution(mesh):
    in_specs = (P(None, None, "grow", "gcol"), P(), P(), P(), P())
    out_specs = P(None, "grow", "gcol")
    return jax.shard_map(shards, mesh=mesh, in_specs=in_specs, out_specs=out_specs, check_vma=False)
```

```python
import functools

import jax
import jax.numpy as jnp
from jax import lax
from jax.experimental import pallas as pl
from jax.experimental.pallas import tpu as pltpu
from jax.sharding import PartitionSpec as P

MESH = pl.DeviceIdType.MESH
SIDE = 4
DEEP = 16
SUB = 32
LAST = 26
LAGS = [[0, 3, 6, 9, 12, 15], [0, 3, 6, 10]]
ROWS = 512

TREES = [
    {
        (1, 0): (0, 1), (1, 3): (1, 0), (2, 3): (0, 3), (2, 1): (0, 3), (0, 1): (0, 3), (1, 2): (0, 3),
        (0, 3): (0, 3), (3, 3): (3, 0), (3, 0): (0, 1), (2, 2): (3, 0), (3, 2): (0, 3), (1, 1): (0, 3),
        (0, 2): (3, 0), (2, 0): (3, 0), (3, 1): (0, 3),
    },
    {
        (1, 0): (1, 0), (3, 0): (3, 0), (2, 0): (1, 0), (1, 2): (0, 2), (3, 1): (0, 1), (3, 3): (0, 3),
        (1, 1): (0, 3), (1, 3): (0, 1), (2, 3): (0, 3), (3, 2): (0, 1), (2, 1): (3, 0), (0, 3): (1, 0),
        (0, 1): (1, 0), (0, 2): (3, 0), (2, 2): (1, 0),
    },
]
SPLIT = 14
STEPS = [(1, 0), (3, 0), (0, 1), (0, 3), (0, 2), (2, 0)]


def children_of(tree, node):
    return [s for s in STEPS if tree.get(((node[0] + s[0]) % SIDE, (node[1] + s[1]) % SIDE)) == s]


def node_depth(tree, node):
    depth = 0
    while node != (0, 0):
        step = tree[node]
        node = ((node[0] - step[0]) % SIDE, (node[1] - step[1]) % SIDE)
        depth += 1
    return depth


NODES = [(px, py) for px in range(SIDE) for py in range(SIDE)]
ROOT_FANS = [children_of(t, (0, 0)) for t in TREES]
FAN = max(len(children_of(t, n)) for t in TREES for n in NODES if n != (0, 0))


def pick(place, values):
    shift = max(max(values).bit_length(), 1)
    per = 31 // shift
    result = jnp.int32(0)
    for start in range(0, len(values), per):
        part = values[start:start + per]
        word = sum(v << (shift * n) for n, v in enumerate(part))
        if word:
            here = (place >= start) & (place < start + per)
            offset = jnp.where(here, place - start, 0) * shift
            result = result + jnp.where(here, (word >> offset) & ((1 << shift) - 1), 0)
    return result


def turn(step, times):
    for _ in range(times):
        step = ((-step[1]) % SIDE, step[0] % SIDE)
    return step


def piece(i):
    s = (i * 11) >> 5
    return s, i - 3 * s


def slot_of(s, way, core):
    if way == 0:
        return jnp.where(s == 0, core, 4 * s - 2 + core)
    return jnp.where(s == 0, core, jnp.where(s == 8, 30 + core, 4 * s + core))


def far_part(way, sub, core):
    return (sub == 2 * way) | ((sub == 1) & (core == way))


def kernel(x_hbm, index_hbm, energy_hbm, out_ref, left_ref, rhs_ref, rows_buf, cols_buf, rhs, wcol, index_ref, energy_ref, ibuf,
           isem, zsend, zrecv, dsend, drecv, csend, crecv):
    g = lax.axis_index("grow")
    gc = lax.axis_index("gcol")
    x, y, z, c = g // SIDE, g % SIDE, gc // 2, gc % 2
    dx, dy = (x - z // SIDE + SIDE) % SIDE, (y - z % SIDE + SIDE) % SIDE
    is_root = (dx == 0) & (dy == 0)

    parts = [(x_hbm.at[SUB * k:SUB * (k + 1), 512 * h:512 * (h + 1)], rows_buf.at[3 * c + k, h])
             for k in range(3) for h in range(2)]
    parts += [(index_hbm, index_ref), (energy_hbm, energy_ref)]
    loads = [pltpu.make_async_copy(src, dst, isem.at[max(n - 5, 0)]) for n, (src, dst) in enumerate(parts)]
    for load in loads[:6]:
        load.start()

    def grow_at(step):
        return ((x + step[0]) % SIDE) * SIDE + (y + step[1]) % SIDE

    def dev(grow, gcol):
        return {"grow": grow, "gcol": gcol}

    ends = [((z + 1) % DEEP) * 2 + c, ((z + DEEP - 1) % DEEP) * 2 + c]
    sibling = dev(g, z * 2 + 1 - c)

    barrier = pltpu.get_barrier_semaphore()
    others = [dev(g, ends[0]), dev(g, ends[1]), sibling]
    others += [dev(grow_at(s), z * 2 + k) for s in STEPS for k in range(2)]
    for other in others:
        pl.semaphore_signal(barrier, inc=1, device_id=other, device_id_type=MESH)
    for load in loads[6:]:
        load.start()

    lags, fans, kids = [[], []], [[], []], [[], []]

    def find_roles():
        px, py = dx, dy
        for tree in range(4):
            place = px * SIDE + py
            for kind, table in enumerate(TREES):
                lags[kind].append(pick(place, [LAGS[kind][node_depth(table, n)] for n in NODES]))
                lists = [children_of(table, n) if n != (0, 0) else [] for n in NODES]
                fans[kind].append(pick(place, [len(v) for v in lists]))
                mine = []
                for n in range(FAN):
                    codes = [STEPS.index(v[n]) if n < len(v) else 0 for v in lists]
                    code = pick(place, codes)
                    chip = jnp.int32(0)
                    for k in sorted(set(codes)):
                        chip = jnp.where(code == k, grow_at(turn(STEPS[k], tree)), chip)
                    mine.append(chip)
                kids[kind].append(mine)
            px, py = py, (SIDE - px) % SIDE

    def arrival(ref, sem):
        pltpu.make_async_copy(ref, ref, sem).wait()

    def zcopy(way, i):
        s, sub = piece(i)
        return pltpu.make_async_remote_copy(
            src_ref=rows_buf.at[3 * slot_of(s, way, c) + sub],
            dst_ref=rows_buf.at[3 * slot_of(s + 1, way, c) + sub],
            send_sem=zsend.at[0], recv_sem=zrecv.at[way, i],
            device_id=dev(g, ends[way]), device_id_type=MESH)

    def dcopy(slot, sub):
        return pltpu.make_async_remote_copy(
            src_ref=rows_buf.at[3 * slot + sub], dst_ref=rows_buf.at[3 * slot + sub],
            send_sem=dsend.at[0], recv_sem=drecv.at[(slot + 2) >> 3],
            device_id=sibling, device_id_type=MESH)

    def root_copies(kind, way, i):
        s, sub = piece(i)
        slot = slot_of(s, way, c)
        tree = 2 * way + c
        copies = []
        for n, step in enumerate(ROOT_FANS[kind]):
            chip = jnp.where(c == 0, grow_at(turn(step, 2 * way)), grow_at(turn(step, 2 * way + 1)))
            for half in range(2):
                copies.append(pltpu.make_async_remote_copy(
                    src_ref=rows_buf.at[3 * slot + sub, half],
                    dst_ref=cols_buf.at[3 * slot + sub],
                    send_sem=csend.at[kind, tree, 2 * n + half], recv_sem=crecv.at[tree, i],
                    device_id=dev(chip, z * 2 + half), device_id_type=MESH))
        return copies

    def ccopy(kind, tree, i, n):
        s, sub = piece(i)
        slot = slot_of(s, tree // 2, tree % 2)
        return pltpu.make_async_remote_copy(
            src_ref=cols_buf.at[3 * slot + sub], dst_ref=cols_buf.at[3 * slot + sub],
            send_sem=csend.at[kind, tree, n], recv_sem=crecv.at[tree, i],
            device_id=dev(kids[kind][tree][n], gc), device_id_type=MESH)

    def z_turn(i, own=False):
        s, sub = piece(i)
        far = [far_part(way, sub, c) for way in range(2)]
        for way in range(2):
            if not own:
                @pl.when((s < 8) | far[way])
                def _():
                    zcopy(way, i - 3).wait_recv()

            @pl.when((s < 7) | ((s == 7) & far[way]))
            def _():
                zcopy(way, i).start()

        @pl.when(is_root)
        def _():
            for kind in range(2):
                @pl.when((i <= SPLIT) if kind == 0 else (i > SPLIT))
                def _():
                    for way in range(1 if own else 2):
                        if kind == 0:
                            for copy in root_copies(kind, way, i):
                                copy.start()
                        else:
                            @pl.when((s < 8) | far[way])
                            def _():
                                for copy in root_copies(kind, way, i):
                                    copy.start()

        for way in range(1 if own else 2):
            @pl.when((s < 8) | far[way])
            def _():
                dcopy(slot_of(s, way, c), sub).start()

    def c_turn(kind, i):
        for tree in range(4):
            j = i - lags[kind][tree]
            if kind == 0:
                ok = (j >= 3 * (tree // 2)) & (j <= SPLIT)
            else:
                s, sub = piece(j)
                ok = (j > SPLIT) & ((s < 8) | ((j <= LAST) & far_part(tree // 2, sub, tree % 2)))

            @pl.when(ok)
            def _():
                ccopy(kind, tree, j, 0).wait_recv()

                def pass_on(n):
                    @pl.when(fans[kind][tree] > n)
                    def _():
                        ccopy(kind, tree, j, n).start()
                        if n + 1 < FAN:
                            pass_on(n + 1)

                pass_on(0)

    def drain(kind):
        def sent(tree, n, more):
            count = SPLIT + 1 - 3 * more if kind == 0 else 23 - SPLIT + more
            arrival(cols_buf.at[0:count], csend.at[kind, tree, n])

        @pl.when(is_root)
        def _():
            for way in range(2):
                for core in range(2):
                    @pl.when(c == core)
                    def _():
                        for n in range(2 * len(ROOT_FANS[kind])):
                            sent(2 * way + core, n, way if kind == 0 else 1 + (way == core))

        @pl.when(jnp.logical_not(is_root))
        def _():
            for tree in range(4):
                way, core = tree // 2, tree % 2
                for n in range(FAN):
                    @pl.when(fans[kind][tree] > n)
                    def _():
                        sent(tree, n, way if kind == 0 else 1 + (way == core))

    def drain_rows():
        arrival(rows_buf.at[0:45], zsend.at[0])
        arrival(rows_buf.at[0:48], dsend.at[0])

    def weights(j):
        lanes = pl.ds(pl.multiple_of(j * 128, 128), 128)

        def look(first, index):
            low, high = index & 127, index >> 7
            value = jnp.zeros((8, 128), jnp.float32)
            for r in range(16):
                row = jnp.broadcast_to(energy_ref[first + r:first + r + 1, :], (8, 128))
                value = jnp.where(high == r, jnp.take_along_axis(row, low, axis=1), value)
            return value

        @pl.when(j == 0)
        def _():
            for load in loads[6:]:
                load.wait()
            ibuf[...] = jnp.zeros_like(ibuf)
            ibuf[0, 0:3, :] = index_ref[0:3, :]
            ibuf[1, 0:3, :] = index_ref[3:6, :]

        w = 2.0 / (look(0, ibuf[0, :, lanes]) - look(16, ibuf[1, :, lanes]))
        for k in range(3):
            wcol[k, lanes, :] = jnp.broadcast_to(w[k:k + 1, :], (128, 128)).T

    def build(first, count, rhs):
        def fill(load):
            @pl.loop(0, count)
            def _(n):
                q = first + n
                s, way, core = (q + 2) // 4, ((q + 2) % 4) // 2, q % 2
                chip = (z + jnp.where(way == 1, s, DEEP - s)) % DEEP
                band = pl.multiple_of((2 * chip + core) * 16, 16)
                base = n * 96
                for k in range(3):
                    w = wcol[k, pl.ds(band, 16), :]
                    w = jnp.concatenate([w] * 4, axis=1)
                    re = (load(q, k, 0).astype(jnp.float32) * w).astype(jnp.bfloat16)
                    im = (load(q, k, 16).astype(jnp.float32) * w).astype(jnp.bfloat16)
                    top = pl.ds(pl.multiple_of(base + 32 * k, 16), 16)
                    low = pl.ds(pl.multiple_of(base + 32 * k + 16, 16), 16)
                    rhs[top, 0:512] = re
                    rhs[low, 0:512] = im
                    rhs[top, 512:1024] = -im
                    rhs[low, 512:1024] = re

        arrival(rows_buf.at[0:3 * count // 2], drecv.at[(first + 2) >> 3])

        @pl.when(is_root)
        def _():
            fill(lambda q, k, r: rows_buf[3 * q + k, c, r:r + 16, :])

        @pl.when(jnp.logical_not(is_root))
        def _():
            fill(lambda q, k, r: cols_buf[3 * q + k, r:r + 16, :])

    def block(first, count, r, fresh):
        at = pl.ds(pl.multiple_of(r * ROWS, ROWS), ROWS)
        left = rows_buf[3 * first:3 * (first + count), r].reshape(count * 96, ROWS)
        value = lax.dot_general(left, rhs[0:count * 96, :], (((0,), (0,)), ((), ())),
                                preferred_element_type=jnp.float32)
        for part in range(2):
            if fresh:
                out_ref[part, at, :] = value[:, part * 512:(part + 1) * 512]
            else:
                out_ref[part, at, :] += value[:, part * 512:(part + 1) * 512]

    blocks = 1024 // ROWS
    groups = [(0, 6), (6, 8), (14, 8), (22, 8), (30, 2)]
    depth0, depth1 = LAGS[0][-1], LAGS[1][-1]

    def ready(last_s):
        i = 3 * last_s + 2
        return i + depth0 if i <= SPLIT else max(SPLIT + depth0, i + depth1)

    begins = [ready(s) for s in (1, 3, 5, 7)]
    turns = LAST + depth1 + 1

    arrival(rows_buf.at[pl.ds(3 * c, 3)], isem.at[0])
    pl.semaphore_wait(barrier, len(others))
    for i in range(3):
        z_turn(jnp.int32(i), own=True)
    find_roles()

    @pl.loop(0, turns)
    def _(i):
        @pl.when((i > 2) & (i <= LAST))
        def _():
            z_turn(i)

        @pl.when(jnp.logical_not(is_root))
        def _():
            @pl.when(i <= SPLIT + depth0)
            def _():
                c_turn(0, i)

            @pl.when(i > SPLIT)
            def _():
                c_turn(1, i)

        @pl.when((i >= 4) & (i < 8))
        def _():
            weights(i - 4)

        for n, begin in enumerate(begins):
            first, count = groups[n]

            @pl.when((i >= begin) & (i < begin + blocks))
            def _():
                @pl.when(i == begin)
                def _():
                    build(first, count, rhs)

                block(first, count, i - begin, n == 0)

    drain(0)
    drain_rows()
    first, count = groups[4]
    build(first, count, rhs_ref)
    left_ref[...] = rows_buf[3 * first:3 * (first + count)]
    drain(1)


def finish(sum_ref, left_ref, rhs_ref, out_ref, part_buf, osem):
    def write(r):
        at = pl.ds(pl.multiple_of(r * 256, 256), 256)
        return pltpu.make_async_copy(part_buf.at[:, at], out_ref.at[:, at], osem.at[r])

    for r in range(4):
        left = left_ref[:, r // 2, :, (r % 2) * 256:(r % 2 + 1) * 256].reshape(6 * SUB, 256)
        value = lax.dot_general(left, rhs_ref[...], (((0,), (0,)), ((), ())), preferred_element_type=jnp.float32)
        for part in range(2):
            at = slice(r * 256, (r + 1) * 256)
            part_buf[part, at, :] = sum_ref[part, at, :] + value[:, part * 512:(part + 1) * 512]
        write(r).start()
    for r in range(4):
        write(r).wait()


def shards(pair_matrix, valence_index, conduction_index, valence_energy, conduction_energy):
    x = jnp.swapaxes(pair_matrix, 2, 3).reshape(96, 1024)
    index = jnp.concatenate([valence_index, conduction_index])
    energy = jnp.concatenate([valence_energy, conduction_energy]).reshape(32, 128)
    total, left, right = pl.pallas_call(
        kernel,
        out_shape=[jax.ShapeDtypeStruct((2, 1024, 512), jnp.float32),
                   jax.ShapeDtypeStruct((6, 2, SUB, 512), jnp.bfloat16),
                   jax.ShapeDtypeStruct((6 * SUB, 1024), jnp.bfloat16)],
        in_specs=[pl.BlockSpec(memory_space=pltpu.HBM)] * 3,
        out_specs=[pl.BlockSpec(memory_space=pltpu.VMEM)] * 3,
        scratch_shapes=[
            pltpu.VMEM((96, 2, SUB, 512), jnp.bfloat16),
            pltpu.VMEM((96, SUB, 512), jnp.bfloat16),
            pltpu.VMEM((768, 1024), jnp.bfloat16),
            pltpu.VMEM((3, 512, 128), jnp.float32),
            pltpu.VMEM((6, 512), jnp.int32),
            pltpu.VMEM((32, 128), jnp.float32),
            pltpu.VMEM((2, 8, 512), jnp.int32),
            pltpu.SemaphoreType.DMA((3,)),
            pltpu.SemaphoreType.DMA((1,)),
            pltpu.SemaphoreType.DMA((2, LAST - 2)),
            pltpu.SemaphoreType.DMA((1,)),
            pltpu.SemaphoreType.DMA((5,)),
            pltpu.SemaphoreType.DMA((2, 4, 4)),
            pltpu.SemaphoreType.DMA((4, LAST + 1)),
        ],
        compiler_params=pltpu.CompilerParams(collective_id=0, has_side_effects=True, vmem_limit_bytes=32 << 20),
        cost_estimate=pl.CostEstimate(flops=6 << 30, bytes_accessed=4 << 20, transcendentals=0),
        name="chi",
    )(x, index, energy)
    return pl.pallas_call(
        finish,
        out_shape=jax.ShapeDtypeStruct((2, 1024, 512), jnp.float32),
        in_specs=[pl.BlockSpec(memory_space=pltpu.VMEM)] * 3,
        out_specs=pl.BlockSpec(memory_space=pl.ANY),
        scratch_shapes=[pltpu.VMEM((2, 1024, 512), jnp.float32), pltpu.SemaphoreType.DMA((4,))],
        compiler_params=pltpu.CompilerParams(vmem_limit_bytes=16 << 20),
        name="finish",
    )(total, left, right)


def solution(mesh):
    in_specs = (P(None, None, "grow", "gcol"), P(), P(), P(), P())
    out_specs = P(None, "grow", "gcol")
    return jax.shard_map(shards, mesh=mesh, in_specs=in_specs, out_specs=out_specs, check_vma=False)
```
